128 devices in a mesh: seq: 8 (over z, core), tp: 16 (over y, x).
Axes of the slice: x: 4, y: 4, z: 4, core: 2. Of those that a mesh axis runs over, the one named last changes fastest.
Arguments:
- hidden: bfloat16 [2048, 4096], P('seq', 'tp'), may hold values from -6 to 6
- expert_ids: int32 [2048, 2], P('seq'), may hold values from 0 to 7, all different within a row; in each aligned block of 256 rows (0 to 255, 256 to 511, ...) at most 96 rows name the same one
- expert_gates: float32 [2048, 2], P('seq'), may hold values from 0.1 to 1
- mamba_gain: float32 [4096], replicated, may hold values from 0.5 to 1.5
- in_x_weight: bfloat16 [4096, 8192], P('seq', 'tp'), may hold values from -0.09375 to 0.09375
- in_z_weight: bfloat16 [4096, 8192], P('seq', 'tp'), may hold values from -0.09375 to 0.09375
- conv_weight: float32 [4, 8192], P(None, 'tp'), may hold values from -3 to 3
- conv_bias: float32 [8192], P('tp'), may hold values from -4 to 4
- x_proj_weight: bfloat16 [8192, 544], P('tp'), may hold values from -1 to 1
- dt_weight: bfloat16 [512, 8192], P(None, 'tp'), may hold values from -0.625 to 0.625
- dt_bias: float32 [8192], P('tp'), may hold values from -5 to 1
- a_log: float32 [16, 8192], P(None, 'tp'), may hold values from -9 to 0
- skip: float32 [8192], P('tp'), may hold values from 0.1 to 4
- ssm_state: float32 [16, 8192], P(None, 'tp'), may hold values from -6 to 6
- out_weight: bfloat16 [8192, 4096], P('tp', 'seq'), may hold values from -0.0625 to 0.0625
- moe_gain: float32 [4096], replicated, may hold values from 0.2 to 2.5
- expert_gate: bfloat16 [8, 4096, 12288], P('seq', None, 'tp'), may hold values from -0.09375 to 0.09375
- expert_up: bfloat16 [8, 4096, 12288], P('seq', None, 'tp'), may hold values from -0.09375 to 0.09375
- expert_down: bfloat16 [8, 12288, 4096], P('seq', 'tp'), may hold values from -0.0546875 to 0.0546875
Outputs:
- mixed: bfloat16 [2048, 4096], P('seq', 'tp')
The draws below stay inside these ranges and needn't reach their ends.
Inputs may be any that keep to these rules, and one draw needn't show every extreme that they name: `expert_ids`: each token names 2 different experts. Among the 256 tokens of one device (aligned blocks) no expert is named by more than 96 tokens, and some block reaches 96.
All inputs are finite; a program needn't handle non-finite values.
Results may differ from the reference program's by a relative error of at most 0.02.
Values may be sent and summed in bfloat16 or wider, within the bound.
A program may use at most 192 MiB of HBM per device.

```python
import math
import jax
import jax.numpy as jnp
import numpy as np
from jax import lax

D = 4096
E = 8192
N = 16
R = 512
CONV = 4
FF = 12288
TOP = 2
TOK_DEV = 256
TOKENS = 2048
EXPERTS = 8
CAP = 96
N_SEQ = 8
N_TP = 16


def draw_dt_bias(key, part):
    key = jax.random.fold_in(key, 11)
    lowest, highest = (0.01, 0.5)
    spread = jax.random.uniform(key, (E,), jnp.float32, jnp.log(lowest), jnp.log(highest))
    return jnp.log(jnp.expm1(jnp.exp(spread)))


def draw_x_proj_weight(key, part):
    key = jax.random.fold_in(key, 13)
    values = jax.random.truncated_normal(key, -6.0, 6.0, (E, R + 2 * N), jnp.float32)
    column = jnp.arange(R + 2 * N, dtype=jnp.int32)
    factor = jnp.where(column < R, 1.0, 0.3).astype(jnp.float32)
    return (values * factor[None, :] / jnp.sqrt(jnp.float32(E))).astype(jnp.bfloat16)


def steps_of(stream_key, dims, split, least, largest):
    level, own = 1.0, jax.random.fold_in(stream_key, 6)
    for dim, shards_of in split:
        draws = jnp.exp(jax.random.uniform(jax.random.fold_in(own, dim), (shards_of,), jnp.float32, least / len(split), largest / len(split)))
        level = level * jnp.repeat(draws, dims[dim] // shards_of).reshape([-1 if axis == dim else 1 for axis in range(len(dims))])
    return level


def assign_block(rng, own, number, rows, count, top, limit, skew):
    ranking = jax.random.permutation(rng, count)
    heavy_load, ordinary = portions_of(count, rows * top, limit, skew, True), portions_of(count, rows * top, limit, skew, False)
    places = jnp.arange(count)

    def named(sizes, turn):
        used = int((sizes > 0).sum())
        fixed = max(1, used // 4)
        shifted = fixed + (places - fixed + turn * (used - fixed)) % max(1, count - fixed)
        return jnp.zeros((count,), jnp.int32).at[ranking[jnp.where(places < fixed, places, shifted)]].set(jnp.asarray(sizes, jnp.int32))

    sizes = jnp.where(number % 4 == 0, named(heavy_load, number // 4), named(ordinary, number - number // 4 - 1))
    mixed = jax.random.permutation(jax.random.fold_in(own, 3), count)
    giver, taker = mixed[0:count // 2 * 2:2], mixed[1:count // 2 * 2:2]
    margin = jnp.minimum(sizes[giver] - 1, limit - sizes[taker]) // 2
    margin = jnp.where((giver == ranking[0]) | (taker == ranking[0]) | (sizes[taker] == 0), 0, jnp.maximum(margin, 0))
    shifted = jax.random.randint(jax.random.fold_in(own, 4), (count // 2,), 0, 1 << 20) % (margin + 1)
    sizes = sizes.at[giver].add(-shifted).at[taker].add(shifted)
    members = jnp.searchsorted(jnp.cumsum(sizes), jnp.arange(rows * top), side="right").astype(jnp.int32)
    listing = members.reshape(top, rows).T
    listing = listing[jax.random.permutation(jax.random.fold_in(own, 1), rows)]
    turn = jax.random.randint(jax.random.fold_in(own, 2), (rows, 1), 0, top)
    return jnp.take_along_axis(listing, (jnp.arange(top)[None, :] + turn) % top, axis=1)


def portions_of(amount, total, bound, skew, full):
    weights = [(1 << 20) // math.isqrt(standing ** skew) + 1 for standing in range(1, amount + 1)]
    largest = bound if full else min(bound, max(-(-total // amount), total * weights[0] // sum(weights)))
    least = 1 if total - largest >= amount - 1 else 0
    holding, surplus = [largest] + [least] * (amount - 1), total - largest - least * (amount - 1)
    while surplus > 0:
        candidates = [i for i in range(1, amount) if holding[i] < largest] or [i for i in range(1, amount) if holding[i] < bound]
        pool, remaining = sum([weights[i] for i in candidates]), surplus
        for i in candidates:
            addition = min(bound - holding[i], max(1, remaining * weights[i] // pool), surplus)
            holding[i] = holding[i] + addition
            surplus = surplus - addition
    return np.array(holding)


def bell_draw(key, shape, scale, bound, cuts=(), kind=jnp.bfloat16):
    loudness = steps_of(key, shape, cuts, -0.22, 0.18) if cuts else 1.0
    result = jax.random.normal(key, shape, jnp.float32) * scale * loudness
    return jnp.minimum(jnp.maximum(result, -bound), bound).astype(kind)


def setup_inputs(seed: int = 0) -> dict:
    keys = jax.random.split(jax.random.key(seed), 20)
    hidden = bell_draw(keys[0], (TOKENS, D), 1.0, 6.0, ((0, 8), (1, 16)))
    expert_ids_keys = jax.random.split(jax.random.fold_in(keys[1], 1), TOKENS // TOK_DEV)
    expert_ids_turns = jax.random.permutation(jax.random.fold_in(keys[1], 3), TOKENS // TOK_DEV)
    expert_ids = jax.vmap(lambda own, number: assign_block(jax.random.fold_in(keys[1], 2), own, number, TOK_DEV, EXPERTS, TOP, CAP, 2))(expert_ids_keys, expert_ids_turns).reshape((TOKENS, TOP))
    expert_gates = jnp.clip(jnp.exp(math.log(1.0) - 2.3025851 * jax.random.uniform(keys[2], (TOKENS, TOP), jnp.float32) ** steps_of(keys[2], (TOKENS, TOP), ((0, 8),), -0.2, 0.2)), 0.1, 1.0)
    mamba_gain = jnp.clip(1.0 + 0.1 * jax.random.normal(keys[3], (D,), jnp.float32), 0.5, 1.5)
    in_x_weight = bell_draw(keys[4], (D, E), D ** -0.5, 0.09375, ((0, 8), (1, 16)))
    in_z_weight = bell_draw(keys[5], (D, E), D ** -0.5, 0.09375, ((0, 8), (1, 16)))
    conv_weight = bell_draw(keys[6], (CONV, E), CONV ** -0.5, 3.0, ((1, 16),), jnp.float32)
    conv_bias = bell_draw(keys[7], (E,), 0.3, 4.0, ((0, 16),), jnp.float32)
    x_proj_weight = draw_x_proj_weight(jax.random.fold_in(keys[19], 71), 0)
    dt_weight = bell_draw(keys[9], (R, E), (R // 6) ** -0.5, 0.625, ((1, 16),))
    dt_bias = draw_dt_bias(jax.random.fold_in(keys[19], 71), 0)
    a_log = jnp.clip(-9.0 + 9.0 * jax.random.uniform(keys[11], (N, E), jnp.float32) ** steps_of(keys[11], (N, E), ((1, 16),), -0.2, 0.2), -9.0, 0.0)
    skip = jnp.clip(jnp.exp(math.log(4.0) - 3.6888794 * jax.random.uniform(keys[12], (E,), jnp.float32) ** steps_of(keys[12], (E,), ((0, 16),), -0.2, 0.2)), 0.1, 4.0)
    ssm_state = bell_draw(keys[13], (N, E), 1.0, 6.0, ((1, 16),), jnp.float32)
    out_weight = bell_draw(keys[14], (E, D), E ** -0.5, 0.0625, ((0, 16), (1, 8)))
    moe_gain = jnp.clip(jnp.exp(jax.random.uniform(keys[15], (D,), jnp.float32, math.log(0.2), math.log(2.5))), 0.2, 2.5)
    expert_gate = bell_draw(keys[16], (EXPERTS, D, FF), D ** -0.5, 0.09375, ((0, 8), (2, 16)))
    expert_up = bell_draw(keys[17], (EXPERTS, D, FF), D ** -0.5, 0.09375, ((0, 8), (2, 16)))
    expert_down = bell_draw(keys[18], (EXPERTS, FF, D), FF ** -0.5, 0.0546875, ((0, 8), (1, 16)))
    return dict(hidden=hidden, expert_ids=expert_ids, expert_gates=expert_gates, mamba_gain=mamba_gain, in_x_weight=in_x_weight, in_z_weight=in_z_weight, conv_weight=conv_weight, conv_bias=conv_bias, x_proj_weight=x_proj_weight, dt_weight=dt_weight, dt_bias=dt_bias, a_log=a_log, skip=skip, ssm_state=ssm_state, out_weight=out_weight, moe_gain=moe_gain, expert_gate=expert_gate, expert_up=expert_up, expert_down=expert_down)


EPS = 1e-06

def rms_scale(values, gain):
    wide = values.astype(jnp.float32)
    mean_square = lax.optimization_barrier(jnp.mean(wide * wide, axis=-1, keepdims=True))
    return wide * lax.rsqrt(mean_square + EPS) * gain

def reference(hidden, expert_ids, expert_gates, mamba_gain, in_x_weight, in_z_weight, conv_weight, conv_bias, x_proj_weight, dt_weight, dt_bias, a_log, skip, ssm_state, out_weight, moe_gain, expert_gate, expert_up, expert_down):
    normed = rms_scale(hidden, mamba_gain).astype(jnp.bfloat16)
    x_inner = jnp.dot(normed, in_x_weight, preferred_element_type=jnp.float32).astype(jnp.bfloat16)
    z_inner = jnp.dot(normed, in_z_weight, preferred_element_type=jnp.float32).astype(jnp.bfloat16)
    leading = jnp.zeros((CONV - 1, E), jnp.bfloat16)
    conv_input = jnp.concatenate([leading, x_inner], 0).astype(jnp.float32)
    conv_sum = conv_bias
    for tap in range(CONV):
        conv_sum = conv_sum + conv_weight[tap] * conv_input[tap:tap + TOKENS]
    inner_u = jax.nn.silu(conv_sum).astype(jnp.bfloat16)
    projected = jnp.dot(inner_u, x_proj_weight, preferred_element_type=jnp.float32)
    dt_low = projected[:, :R].astype(jnp.bfloat16)
    b_mat = projected[:, R:R + N]
    c_mat = projected[:, R + N:]
    step_size = jax.nn.softplus(jnp.dot(dt_low, dt_weight, preferred_element_type=jnp.float32) + dt_bias)
    rate = -jnp.exp(a_log)
    u_wide = inner_u.astype(jnp.float32)

    def advance(state, inputs):
        step_now, b_now, c_now, u_now = inputs
        state = jnp.exp(step_now[None, :] * rate) * state + b_now[:, None] * (step_now * u_now)[None, :]
        return (state, lax.optimization_barrier(jnp.sum(c_now[:, None] * state, 0)))
    _, scanned = lax.scan(advance, ssm_state, (step_size, b_mat, c_mat, u_wide))
    inner_y = scanned + skip * u_wide
    gated = (inner_y * jax.nn.silu(z_inner.astype(jnp.float32))).astype(jnp.bfloat16)
    residual = (hidden.astype(jnp.float32) + jnp.dot(gated, out_weight, preferred_element_type=jnp.float32)).astype(jnp.bfloat16)
    moe_in = rms_scale(residual, moe_gain).astype(jnp.bfloat16)
    block_ids = expert_ids.reshape(N_SEQ, TOK_DEV * TOP)
    choose = (block_ids[:, :, None] == jnp.arange(EXPERTS, dtype=jnp.int32)[None, None, :]).astype(jnp.int32)
    slot = lax.optimization_barrier(jnp.sum(jnp.cumsum(choose, 1) * choose, 2)) - 1
    source = jnp.arange(N_SEQ, dtype=jnp.int32)[:, None]
    target = (block_ids * (N_SEQ * CAP) + source * CAP + slot).astype(jnp.int32)
    token_of = (jnp.arange(TOKENS * TOP, dtype=jnp.int32) // TOP).astype(jnp.int32)
    table = jnp.zeros((EXPERTS * N_SEQ * CAP,), jnp.int32).at[target.reshape(-1)].set(token_of)
    table = table.reshape(EXPERTS, N_SEQ * CAP)

    def one_expert(inputs):
        index, gate_w, up_w, down_w = inputs
        chosen = moe_in[index]
        gate_val = jnp.dot(chosen, gate_w, preferred_element_type=jnp.float32)
        up_val = jnp.dot(chosen, up_w, preferred_element_type=jnp.float32)
        active = (jax.nn.silu(gate_val) * up_val).astype(jnp.bfloat16)
        groups = active.astype(jnp.float32).reshape(-1, N_TP, FF // N_TP)
        down_groups = down_w.astype(jnp.float32).reshape(N_TP, FF // N_TP, D)
        partial_sums = jnp.einsum('rjf,jfd->rjd', groups, down_groups)
        rounded = lax.optimization_barrier(partial_sums.astype(jnp.bfloat16))
        return lax.optimization_barrier(jnp.sum(rounded.astype(jnp.float32), 1)).astype(jnp.bfloat16)
    expert_out = lax.map(one_expert, (table, expert_gate, expert_up, expert_down))
    flat_out = expert_out.reshape(EXPERTS * N_SEQ * CAP, D)
    picked = flat_out[target.reshape(TOKENS, TOP)].astype(jnp.float32)
    combined = lax.optimization_barrier(jnp.sum(picked * expert_gates[:, :, None], 1))
    return (residual.astype(jnp.float32) + combined).astype(jnp.bfloat16)
```

```python
import jax
import jax.numpy as jnp
from jax import lax
from jax.experimental import pallas as pl
from jax.experimental.pallas import tpu as pltpu
from jax.sharding import PartitionSpec as P

EPS = 1e-06
LOG2E = 1.4426950408889634
VMEM = pltpu.VMEM


def rms_scale(values, gain):
    wide = values.astype(jnp.float32)
    mean_square = jnp.mean(wide * wide, axis=-1, keepdims=True)
    return wide * lax.rsqrt(mean_square + EPS) * gain


def softplus(v):
    return jnp.maximum(v, 0.0) + jnp.log1p(jnp.exp(-jnp.abs(v)))


def silu(v):
    return v / (1.0 + jnp.exp(-v))


def spread_b(bc, bt_ref):
    flipped = bc.T
    for g in range(16):
        bt_ref[g, :, 0:16] = flipped[0:16, 16 * g : 16 * g + 16]


def block_c(bc):
    row = lax.broadcasted_iota(jnp.int32, (128, 256), 0)
    col = lax.broadcasted_iota(jnp.int32, (128, 256), 1)
    tile = jnp.where(row - 16 == col % 16, 1.0, 0.0).astype(jnp.bfloat16)
    wide = jnp.dot(bc.astype(jnp.bfloat16), tile, preferred_element_type=jnp.float32)
    row = lax.broadcasted_iota(jnp.int32, (256, 256), 0)
    col = lax.broadcasted_iota(jnp.int32, (256, 256), 1)
    return jnp.where(row % 16 == col // 16, wide, 0.0).astype(jnp.bfloat16)


def run_states(step_ref, dtx_ref, bt_ref, rate, start, keep):
    def group(g, state):
        rows = pl.ds(pl.multiple_of(g * 16, 16), 16)
        step = step_ref[rows, :]
        dtx = dtx_ref[rows, :]
        b = bt_ref[g]
        for j in range(16):
            decay = jnp.exp2(step[j : j + 1, :] * rate)
            state = decay * state + b[:, j : j + 1] * dtx[j : j + 1, :]
            if keep is not None:
                keep[pl.ds(pl.multiple_of(g * 256 + 16 * j, 16), 16), :] = state.astype(jnp.bfloat16)
        return state

    return lax.fori_loop(0, 16, group, start)


def scan_local(low, bc, u, dt_weight, dt_bias, a_log, step, dtx, last, decay, bt):
    v = jnp.dot(low[...].astype(jnp.bfloat16), dt_weight[...], preferred_element_type=jnp.float32)
    size = softplus(v + dt_bias[...])
    step[...] = size
    dtx[...] = size * u[...].astype(jnp.float32)
    spread_b(bc[...], bt)
    rate = jnp.exp(a_log[...]) * (-LOG2E)
    last[...] = run_states(step, dtx, bt, rate, jnp.zeros((16, 512), jnp.float32), None)
    decay[...] = jnp.exp2(rate * jnp.sum(size, axis=0, keepdims=True))


def scan_final(bc, step, dtx, u, z, skip, a_log, start, gated, bt, kept, y):
    spread_b(bc[...], bt)
    rate = jnp.exp(a_log[...]) * (-LOG2E)
    run_states(step, dtx, bt, rate, start[...], kept)
    c = block_c(bc[...])
    for g in range(16):
        y[16 * g : 16 * g + 16, :] = jnp.dot(
            c[16 * g : 16 * g + 16, :], kept[256 * g : 256 * g + 256, :], preferred_element_type=jnp.float32
        )
    inner = y[...] + skip[...] * u[...].astype(jnp.float32)
    gated[...] = (inner * silu(z[...].astype(jnp.float32))).astype(jnp.bfloat16)


def f32(*shape):
    return jax.ShapeDtypeStruct(shape, jnp.float32)


def bf16(*shape):
    return jax.ShapeDtypeStruct(shape, jnp.bfloat16)


def call(kernel, outs, scratch, *args):
    vm = pl.BlockSpec(memory_space=pltpu.VMEM)
    return pl.pallas_call(
        kernel,
        out_shape=outs,
        in_specs=[vm] * len(args),
        out_specs=jax.tree.map(lambda _: vm, outs),
        scratch_shapes=scratch,
        compiler_params=pltpu.CompilerParams(vmem_limit_bytes=40 << 20),
    )(*args)


def expert_apply(received, moe_gain, expert_gate, expert_up, expert_down):
    sources, count, width = received.shape
    flat_rows = received.reshape(sources * count, width)
    normed = rms_scale(flat_rows, moe_gain).astype(jnp.bfloat16)
    gate_val = jnp.dot(normed, expert_gate[0], preferred_element_type=jnp.float32)
    up_val = jnp.dot(normed, expert_up[0], preferred_element_type=jnp.float32)
    active = (jax.nn.silu(gate_val) * up_val).astype(jnp.bfloat16)
    partial_out = jnp.dot(active, expert_down[0], preferred_element_type=jnp.float32)
    partial_out = partial_out.reshape(sources, count, width)
    return lax.psum_scatter(partial_out.astype(jnp.bfloat16), "tp", scatter_dimension=2, tiled=True)


def local(
    hidden,
    expert_ids,
    expert_gates,
    mamba_gain,
    in_x_weight,
    in_z_weight,
    conv_weight,
    conv_bias,
    x_proj_weight,
    dt_weight,
    dt_bias,
    a_log,
    skip,
    ssm_state,
    out_weight,
    moe_gain,
    expert_gate,
    expert_up,
    expert_down,
):
    tokens_here, slice_width = hidden.shape
    taps, channels = conv_weight.shape
    s = lax.axis_index("seq")
    full_hidden = lax.all_gather(hidden, "tp", axis=1, tiled=True)
    normed = rms_scale(full_hidden, mamba_gain).astype(jnp.bfloat16)
    x_inner = jnp.dot(
        normed, lax.all_gather(in_x_weight, "seq", axis=0, tiled=True), preferred_element_type=jnp.float32
    ).astype(jnp.bfloat16)
    z_inner = jnp.dot(
        normed, lax.all_gather(in_z_weight, "seq", axis=0, tiled=True), preferred_element_type=jnp.float32
    ).astype(jnp.bfloat16)
    previous = lax.ppermute(x_inner[tokens_here - (taps - 1) :], "seq", [(i, i + 1) for i in range(7)])
    conv_input = jnp.concatenate([previous, x_inner], 0).astype(jnp.float32)
    conv_sum = conv_bias
    for tap in range(taps):
        conv_sum = conv_sum + conv_weight[tap] * conv_input[tap : tap + tokens_here]
    inner_u = jax.nn.silu(conv_sum).astype(jnp.bfloat16)
    share = jnp.dot(inner_u, x_proj_weight, preferred_element_type=jnp.float32)
    projected = lax.psum(share.astype(jnp.bfloat16), "tp").astype(jnp.float32)
    low = projected[:, :512]
    bc = jnp.pad(projected[:, 512:], ((0, 0), (0, 96)))
    step, dtx, last, decay = call(
        scan_local,
        [f32(256, 512), f32(256, 512), f32(16, 512), f32(16, 512)],
        [VMEM((16, 16, 128), jnp.float32)],
        low, bc, inner_u, dt_weight, dt_bias[None], a_log,
    )
    both = lax.all_gather(jnp.stack([decay, last]), "seq")
    start = ssm_state
    for k in range(7):
        start = jnp.where(k < s, both[k, 0] * start + both[k, 1], start)
    gated = call(
        scan_final,
        bf16(256, 512),
        [VMEM((16, 16, 128), jnp.float32), VMEM((4096, 512), jnp.bfloat16), VMEM((256, 512), jnp.float32)],
        bc, step, dtx, inner_u, z_inner, skip[None], a_log, start,
    )
    mamba_terms = jnp.dot(
        gated, lax.all_gather(out_weight, "seq", axis=1, tiled=True), preferred_element_type=jnp.float32
    )
    mamba_share = lax.psum_scatter(
        mamba_terms.astype(jnp.bfloat16), "tp", scatter_dimension=1, tiled=True
    ).astype(jnp.float32)
    residual = (hidden.astype(jnp.float32) + mamba_share).astype(jnp.bfloat16)

    experts = jnp.arange(8, dtype=jnp.int32)
    chosen = (expert_ids[:, :, None] == experts).astype(jnp.float32)
    either = jnp.sum(chosen, 1)
    t = jnp.arange(tokens_here)
    before = (t[:, None] > t[None, :]).astype(jnp.bfloat16)
    slot = jnp.dot(before, either.astype(jnp.bfloat16), preferred_element_type=jnp.float32)
    place = slot[:, :, None] == jnp.arange(96, dtype=jnp.float32)
    pick = [
        jnp.where(place & (chosen[:, k, :, None] > 0), 1.0, 0.0).astype(jnp.bfloat16).reshape(256, 768)
        for k in range(2)
    ]
    outgoing = (
        lax.dot_general(pick[0] + pick[1], residual, (((0,), (0,)), ((), ())), preferred_element_type=jnp.float32)
        .astype(jnp.bfloat16)
        .reshape(8, 96, slice_width)
    )
    whole_rows = lax.all_gather(
        lax.all_to_all(outgoing, "seq", split_axis=0, concat_axis=0, tiled=True), "tp", axis=2, tiled=True
    )
    results = expert_apply(whole_rows, moe_gain, expert_gate, expert_up, expert_down)
    returned = lax.all_to_all(results, "seq", split_axis=0, concat_axis=0, tiled=True).reshape(768, slice_width)
    combined = sum(
        expert_gates[:, k : k + 1] * jnp.dot(pick[k], returned, preferred_element_type=jnp.float32) for k in range(2)
    )
    return (residual.astype(jnp.float32) + combined).astype(jnp.bfloat16)


def solution(mesh):
    placed = (
        P("seq", "tp"),
        P("seq", None),
        P("seq", None),
        P(),
        P("seq", "tp"),
        P("seq", "tp"),
        P(None, "tp"),
        P("tp"),
        P("tp", None),
        P(None, "tp"),
        P("tp"),
        P(None, "tp"),
        P("tp"),
        P(None, "tp"),
        P("tp", "seq"),
        P(),
        P("seq", None, "tp"),
        P("seq", None, "tp"),
        P("seq", "tp", None),
    )
    return jax.shard_map(local, mesh=mesh, in_specs=placed, out_specs=P("seq", "tp"), check_vma=False)
```

```python
import jax
import jax.numpy as jnp
from jax import lax
from jax.experimental import pallas as pl
from jax.experimental.pallas import tpu as pltpu
from jax.sharding import PartitionSpec as P

EPS = 1e-06
LOG2E = 1.4426950408889634
VMEM = pltpu.VMEM


def rms_scale(values, gain):
    wide = values.astype(jnp.float32)
    mean_square = jnp.mean(wide * wide, axis=-1, keepdims=True)
    return wide * lax.rsqrt(mean_square + EPS) * gain


def softplus(v):
    return jnp.maximum(v, 0.0) + jnp.log1p(jnp.exp(-jnp.abs(v)))


def silu(v):
    return v / (1.0 + jnp.exp(-v))


def spread_b(bc, bt_ref):
    flipped = bc.T
    for g in range(16):
        bt_ref[g, :, 0:16] = flipped[0:16, 16 * g : 16 * g + 16]


def block_c(bc):
    row = lax.broadcasted_iota(jnp.int32, (128, 256), 0)
    col = lax.broadcasted_iota(jnp.int32, (128, 256), 1)
    tile = jnp.where(row - 16 == col % 16, 1.0, 0.0).astype(jnp.bfloat16)
    wide = jnp.dot(bc.astype(jnp.bfloat16), tile, preferred_element_type=jnp.float32)
    row = lax.broadcasted_iota(jnp.int32, (256, 256), 0)
    col = lax.broadcasted_iota(jnp.int32, (256, 256), 1)
    return jnp.where(row % 16 == col // 16, wide, 0.0).astype(jnp.bfloat16)


def run_states(step_ref, dtx_ref, bt_ref, rate, start, keep):
    def group(g, state):
        rows = pl.ds(pl.multiple_of(g * 16, 16), 16)
        step = step_ref[rows, :]
        dtx = dtx_ref[rows, :]
        b = bt_ref[g]
        for j in range(16):
            decay = jnp.exp2(step[j : j + 1, :] * rate)
            state = decay * state + b[:, j : j + 1] * dtx[j : j + 1, :]
            if keep is not None:
                keep[pl.ds(pl.multiple_of(g * 256 + 16 * j, 16), 16), :] = state.astype(jnp.bfloat16)
        return state

    return lax.fori_loop(0, 16, group, start)


def scan_local(low, bc, u, dt_weight, dt_bias, a_log, step, dtx, last, decay, bt):
    v = jnp.dot(low[...].astype(jnp.bfloat16), dt_weight[...], preferred_element_type=jnp.float32)
    size = softplus(v + dt_bias[...])
    step[...] = size
    dtx[...] = size * u[...].astype(jnp.float32)
    spread_b(bc[...], bt)
    rate = jnp.exp(a_log[...]) * (-LOG2E)
    last[...] = run_states(step, dtx, bt, rate, jnp.zeros((16, 512), jnp.float32), None)
    decay[...] = jnp.exp2(rate * jnp.sum(size, axis=0, keepdims=True))


def scan_final(bc, step, dtx, u, z, skip, a_log, start, gated, bt, kept, y):
    spread_b(bc[...], bt)
    rate = jnp.exp(a_log[...]) * (-LOG2E)
    run_states(step, dtx, bt, rate, start[...], kept)
    c = block_c(bc[...])
    for g in range(16):
        y[16 * g : 16 * g + 16, :] = jnp.dot(
            c[16 * g : 16 * g + 16, :], kept[256 * g : 256 * g + 256, :], preferred_element_type=jnp.float32
        )
    inner = y[...] + skip[...] * u[...].astype(jnp.float32)
    gated[...] = (inner * silu(z[...].astype(jnp.float32))).astype(jnp.bfloat16)


def f32(*shape):
    return jax.ShapeDtypeStruct(shape, jnp.float32)


def bf16(*shape):
    return jax.ShapeDtypeStruct(shape, jnp.bfloat16)


def call(kernel, outs, scratch, *args):
    vm = pl.BlockSpec(memory_space=pltpu.VMEM)
    return pl.pallas_call(
        kernel,
        out_shape=outs,
        in_specs=[vm] * len(args),
        out_specs=jax.tree.map(lambda _: vm, outs),
        scratch_shapes=scratch,
        compiler_params=pltpu.CompilerParams(vmem_limit_bytes=40 << 20),
    )(*args)


MESH = pl.DeviceIdType.MESH


def here():
    s, t = lax.axis_index("seq"), lax.axis_index("tp")
    return s, t, t // 4, t % 4


def remote(src, dst, sems, kind, device):
    return pltpu.make_async_remote_copy(
        src_ref=src,
        dst_ref=dst,
        send_sem=sems[0].at[kind],
        recv_sem=sems[1].at[kind],
        device_id=device,
        device_id_type=MESH,
    )


def slot_of(h, f, g):
    _, _, y, x = here()
    dy, dx = (g, f) if h == 0 else (f, g)
    return (y + dy) % 4 * 4 + (x + dx) % 4


def f_peer(h, d):
    return {"tp": slot_of(h, d, 0)}


def g_peer(h, d):
    return {"tp": slot_of(h, 0, d)}


def greet(seq_peers, pair=False):
    s, t, y, x = here()
    barrier = pltpu.get_barrier_semaphore()
    peers = [g_peer(0, 1), g_peer(0, 3), g_peer(1, 1), g_peer(1, 3)]
    peers += [{"seq": (s + d) % 8} for d in seq_peers]
    for peer in peers:
        pl.semaphore_signal(barrier, inc=1, device_id=peer, device_id_type=MESH)
    pl.semaphore_wait(barrier, len(peers))


def gather_tp(full, halves, sems, first=0):
    def part(h, f, g, piece):
        lo, mid, hi = halves[h]
        a, b = {"h": (lo, hi), "q1": (lo, mid), "q2": (mid, hi)}[piece]
        return full.at[slot_of(h, f, g), a:b, :]

    def move(h, axis, f, piece, out, kind):
        d = 1 if kind in (0, 2) else 3
        if axis == "f":
            ref = part(h, out, 0, piece)
            return remote(ref, ref, (sems[0].at[h], sems[1].at[h]), 16 + kind, f_peer(h, d))
        ref = part(h, f, out, piece)
        return remote(ref, ref, (sems[0].at[h], sems[1].at[h]), f * 4 + kind, g_peer(h, d))

    def send(h, axis, f, kind):
        off = {0: 0, 1: 0, 2: 3, 3: 1}[kind]
        move(h, axis, f, {0: "h", 1: "h", 2: "q1", 3: "q2"}[kind], off, kind).start()

    def arrived(h, axis, f, kind):
        off = {0: 3, 1: 1, 2: 2, 3: 2}[kind]
        move(h, axis, f, {0: "h", 1: "h", 2: "q1", 3: "q2"}[kind], off, kind).wait_recv()

    def sent(h, axis, f, kind):
        off = {0: 0, 1: 0, 2: 3, 3: 1}[kind]
        move(h, axis, f, {0: "h", 1: "h", 2: "q1", 3: "q2"}[kind], off, kind).wait_send()

    def begin(h):
        for kind in (0, 1):
            send(h, "f", 0, kind)
        for kind in (0, 1):
            send(h, "g", 0, kind)

    def second(h):
        for kind, f in ((0, 3), (1, 1)):
            arrived(h, "f", 0, kind)
            send(h, "f", 0, kind + 2)
            send(h, "g", f, 0)
            send(h, "g", f, 1)

    def onward(h, f):
        for kind in (0, 1):
            arrived(h, "g", f, kind)
            send(h, "g", f, kind + 2)

    def third(h):
        for kind in (2, 3):
            arrived(h, "f", 0, kind)
        send(h, "g", 2, 0)
        send(h, "g", 2, 1)

    def last(h):
        for f in range(4):
            for kind in (2, 3):
                arrived(h, "g", f, kind)

    def finish():
        for h in (0, 1):
            for kind in range(4):
                sent(h, "f", 0, kind)
            for f in range(4):
                for kind in range(4):
                    sent(h, "g", f, kind)

    stages = [
        lambda: [begin(h) for h in (0, 1)],
        lambda: [second(h) for h in (0, 1)],
        lambda: [onward(h, 0) for h in (0, 1)],
        lambda: [third(h) for h in (0, 1)],
        lambda: [onward(h, f) for f in (3, 1) for h in (0, 1)],
        lambda: [onward(h, 2) for h in (0, 1)],
        lambda: [last(h) for h in (0, 1)],
    ]
    return stages, finish


def add_to(ref, *others):
    total = ref[...].astype(jnp.float32)
    for other in others:
        total = total + other[...].astype(jnp.float32)
    ref[...] = total.astype(jnp.bfloat16)


def scatter_tp(part, half, quarter, fill, bufs, sems):
    uq, uh, vq, vh = bufs

    def rows(h, piece):
        lo = h * half
        a, b = {"h": (lo, lo + half), "q1": (lo, lo + quarter), "q2": (lo + quarter, lo + half)}[piece]
        return slice(a, b)

    def spot(h, f, g, piece):
        return part.at[slot_of(h, f, g), rows(h, piece), :]

    names = ("q1", "q2", "h", "h")
    offs = (2, 2, 1, 3)

    def u_move(h, f, kind):
        dst = (uq.at[h, f, kind] if kind < 2 else uh.at[h, f, kind - 2])
        src = spot(h, f, offs[kind], names[kind])
        return remote(src, dst, (sems[0].at[h], sems[1].at[h]), f * 4 + kind, g_peer(h, 1 if kind % 2 == 0 else 3))

    def v_move(h, kind):
        dst = (vq.at[h, kind] if kind < 2 else vh.at[h, kind - 2])
        src = spot(h, offs[kind], 0, names[kind])
        return remote(src, dst, (sems[0].at[h], sems[1].at[h]), 16 + kind, f_peer(h, 1 if kind % 2 == 0 else 3))

    def each(fn):
        for h in (0, 1):
            lax.fori_loop(0, 4, lambda f, _, h=h: (fn(h, f), 0)[1], 0)

    def step1(h, f):
        fill(slot_of(h, f, 2), h)
        u_move(h, f, 0).start()
        u_move(h, f, 1).start()

    def made(h, f):
        fill(slot_of(h, f, 1), h)
        fill(slot_of(h, f, 3), h)

    def step2(h, f):
        for kind, g, piece in ((0, 1, "q1"), (1, 3, "q2")):
            u_move(h, f, kind).wait_recv()
            add_to(spot(h, f, g, piece), uq.at[h, f, kind])
            u_move(h, f, kind + 2).start()

    def own(h, f):
        fill(slot_of(h, f, 0), h)

    def step3(h, f):
        u_move(h, f, 2).wait_recv()
        u_move(h, f, 3).wait_recv()
        add_to(spot(h, f, 0, "h"), uh.at[h, f, 0], uh.at[h, f, 1])

    each(step1)
    each(made)
    each(step2)
    each(own)
    for h in (0, 1):
        step3(h, 2)
        v_move(h, 0).start()
        v_move(h, 1).start()
    for f, kind, piece in ((1, 0, "q1"), (3, 1, "q2")):
        for h in (0, 1):
            step3(h, f)
            v_move(h, kind).wait_recv()
            add_to(spot(h, f, 0, piece), vq.at[h, kind])
            v_move(h, kind + 2).start()
    for h in (0, 1):
        step3(h, 0)
    for h in (0, 1):
        v_move(h, 2).wait_recv()
        v_move(h, 3).wait_recv()
        add_to(spot(h, 0, 0, "h"), vh.at[h, 0], vh.at[h, 1])

    def finish():
        def u_sent(h, f):
            for kind in range(4):
                u_move(h, f, kind).wait_send()

        each(u_sent)
        for h in (0, 1):
            for kind in range(4):
                v_move(h, kind).wait_send()

    return finish


def tail(
    gated, hidden, ids, gates, gain, out_w, gate_hbm, up_hbm, down_hbm,
    out,
    gate_w, up_w, down_w, terms, outgoing, full, normed, active, parts, back, resid,
    tq, th, tvq, tvh, pq, ph, pvq, pvh,
    w_sem, t_send, t_recv, g_send, g_recv, p_send, p_recv, a_send, a_recv, b_send, b_recv,
):
    s, t, _, _ = here()
    loads = [
        pltpu.make_async_copy(src.at[0], dst, w_sem.at[i])
        for i, (src, dst) in enumerate(((gate_hbm, gate_w), (up_hbm, up_w), (down_hbm, down_w)))
    ]
    for load in loads:
        load.start()
    greet(range(1, 8))

    def fill_terms(slot, h):
        cols = pl.ds(pl.multiple_of(slot * 256, 256), 256)
        terms[slot, h * 128 : h * 128 + 128, :] = jnp.dot(
            gated[h * 128 : h * 128 + 128, :], out_w[:, cols], preferred_element_type=jnp.float32
        ).astype(jnp.bfloat16)

    terms_done = scatter_tp(terms, 128, 64, fill_terms, (tq, th, tvq, tvh), (t_send, t_recv))
    resid[...] = (hidden[...].astype(jnp.float32) + terms[t].astype(jnp.float32)).astype(jnp.bfloat16)

    lane = lax.broadcasted_iota(jnp.int32, (256, 128), 1)
    either = jnp.where((lane == ids[:, 0:1]) | (lane == ids[:, 1:2]), 1.0, 0.0).astype(jnp.bfloat16)
    row = lax.broadcasted_iota(jnp.int32, (256, 256), 0)
    col = lax.broadcasted_iota(jnp.int32, (256, 256), 1)
    before = jnp.where(row > col, 1.0, 0.0).astype(jnp.bfloat16)
    slots = jnp.dot(before, either, preferred_element_type=jnp.float32)
    column = lax.broadcasted_iota(jnp.int32, (256, 768), 1).astype(jnp.float32)

    def pick(k):
        mine = ids[:, k : k + 1]
        place = jnp.sum(jnp.where(lane == mine, slots, 0.0), axis=1, keepdims=True)
        target = place + 96.0 * mine.astype(jnp.float32)
        return jnp.where(column == target, 1.0, 0.0).astype(jnp.bfloat16)

    outgoing[...] = lax.dot_general(
        pick(0) + pick(1), resid[...], (((0,), (0,)), ((), ())), preferred_element_type=jnp.float32
    ).astype(jnp.bfloat16)

    def mine(ref, k):
        return ref.at[pl.ds(pl.multiple_of(k * 96, 16), 96), :]

    def there(d):
        peer = (s + d) % 8
        return remote(mine(outgoing, peer), mine(full.at[t], s), (a_send, a_recv), d, {"seq": peer})

    for d in range(1, 8):
        there(d).start()
    full[t, pl.ds(pl.multiple_of(s * 96, 16), 96), :] = mine(outgoing, s)[...]
    for d in range(1, 8):
        there(d).wait_recv()

    stages, gathered = gather_tp(full, ((0, 192, 384), (384, 576, 768)), (g_send, g_recv))
    for stage in stages:
        stage()

    def squares(k, total):
        wide = full[k].astype(jnp.float32)
        return total + jnp.sum(wide * wide, axis=1, keepdims=True)

    total = lax.fori_loop(0, 16, squares, jnp.zeros((768, 1), jnp.float32))
    scale = lax.rsqrt(total * (1.0 / 4096.0) + EPS)

    def norm(k, _):
        cols = pl.ds(pl.multiple_of(k * 256, 256), 256)
        normed[:, cols] = (full[k].astype(jnp.float32) * scale * gain[:, cols]).astype(jnp.bfloat16)
        return 0

    lax.fori_loop(0, 16, norm, 0)
    loads[0].wait()
    loads[1].wait()

    def hidden_units(i, _):
        rows = pl.ds(pl.multiple_of(i * 256, 256), 256)
        for j in range(3):
            cols = slice(j * 256, j * 256 + 256)
            a = jnp.dot(normed[rows, :], gate_w[:, cols], preferred_element_type=jnp.float32)
            b = jnp.dot(normed[rows, :], up_w[:, cols], preferred_element_type=jnp.float32)
            active[rows, cols] = (silu(a) * b).astype(jnp.bfloat16)
        return 0

    lax.fori_loop(0, 3, hidden_units, 0)
    loads[2].wait()

    def fill_parts(slot, h):
        cols = pl.ds(pl.multiple_of(slot * 256, 256), 256)
        parts[slot, h * 384 : h * 384 + 384, :] = jnp.dot(
            active[h * 384 : h * 384 + 384, :], down_w[:, cols], preferred_element_type=jnp.float32
        ).astype(jnp.bfloat16)

    parts_done = scatter_tp(parts, 384, 192, fill_parts, (pq, ph, pvq, pvh), (p_send, p_recv))

    def home(d):
        peer = (s + d) % 8
        return remote(mine(parts.at[t], peer), mine(back, s), (b_send, b_recv), d, {"seq": peer})

    for d in range(1, 8):
        home(d).start()
    mine(back, s)[...] = mine(parts.at[t], s)[...]
    for d in range(1, 8):
        home(d).wait_recv()
    total = resid[...].astype(jnp.float32)
    for k in range(2):
        total = total + gates[:, k : k + 1] * jnp.dot(pick(k), back[...], preferred_element_type=jnp.float32)
    out[...] = total.astype(jnp.bfloat16)

    terms_done()
    gathered()
    parts_done()
    for d in range(1, 8):
        there(d).wait_send()
        home(d).wait_send()


def call_tail(gated, hidden, ids, gates, gain, out_w, gate_w, up_w, down_w):
    vm, hbm = pl.BlockSpec(memory_space=pltpu.VMEM), pl.BlockSpec(memory_space=pl.ANY)
    b16 = jnp.bfloat16
    dma = pltpu.SemaphoreType.DMA

    def bufs(half):
        q = half // 2
        return [VMEM((2, 4, 2, q, 256), b16), VMEM((2, 4, 2, half, 256), b16), VMEM((2, 2, q, 256), b16), VMEM((2, 2, half, 256), b16)]

    return pl.pallas_call(
        tail,
        out_shape=bf16(256, 256),
        in_specs=[vm] * 6 + [hbm] * 3,
        out_specs=vm,
        scratch_shapes=[
            VMEM((4096, 768), b16), VMEM((4096, 768), b16), VMEM((768, 4096), b16),
            VMEM((16, 256, 256), b16), VMEM((768, 256), b16), VMEM((16, 768, 256), b16), VMEM((768, 4096), b16),
            VMEM((768, 768), b16), VMEM((16, 768, 256), b16), VMEM((768, 256), b16), VMEM((256, 256), b16),
            *bufs(128), *bufs(384),
            dma((3,)), dma((2, 20)), dma((2, 20)), dma((2, 20)), dma((2, 20)), dma((2, 20)), dma((2, 20)),
            dma((8,)), dma((8,)), dma((8,)), dma((8,)),
        ],
        compiler_params=pltpu.CompilerParams(collective_id=1, has_side_effects=True, vmem_limit_bytes=60 << 20),
    )(gated, hidden, ids, gates, gain, out_w, gate_w, up_w, down_w)


def local(
    hidden,
    expert_ids,
    expert_gates,
    mamba_gain,
    in_x_weight,
    in_z_weight,
    conv_weight,
    conv_bias,
    x_proj_weight,
    dt_weight,
    dt_bias,
    a_log,
    skip,
    ssm_state,
    out_weight,
    moe_gain,
    expert_gate,
    expert_up,
    expert_down,
):
    tokens_here, slice_width = hidden.shape
    taps, channels = conv_weight.shape
    s = lax.axis_index("seq")
    full_hidden = lax.all_gather(hidden, "tp", axis=1, tiled=True)
    normed = rms_scale(full_hidden, mamba_gain).astype(jnp.bfloat16)
    x_inner = jnp.dot(
        normed, lax.all_gather(in_x_weight, "seq", axis=0, tiled=True), preferred_element_type=jnp.float32
    ).astype(jnp.bfloat16)
    z_inner = jnp.dot(
        normed, lax.all_gather(in_z_weight, "seq", axis=0, tiled=True), preferred_element_type=jnp.float32
    ).astype(jnp.bfloat16)
    previous = lax.ppermute(x_inner[tokens_here - (taps - 1) :], "seq", [(i, i + 1) for i in range(7)])
    conv_input = jnp.concatenate([previous, x_inner], 0).astype(jnp.float32)
    conv_sum = conv_bias
    for tap in range(taps):
        conv_sum = conv_sum + conv_weight[tap] * conv_input[tap : tap + tokens_here]
    inner_u = jax.nn.silu(conv_sum).astype(jnp.bfloat16)
    share = jnp.dot(inner_u, x_proj_weight, preferred_element_type=jnp.float32)
    projected = lax.psum(share.astype(jnp.bfloat16), "tp").astype(jnp.float32)
    low = projected[:, :512]
    bc = jnp.pad(projected[:, 512:], ((0, 0), (0, 96)))
    step, dtx, last, decay = call(
        scan_local,
        [f32(256, 512), f32(256, 512), f32(16, 512), f32(16, 512)],
        [VMEM((16, 16, 128), jnp.float32)],
        low, bc, inner_u, dt_weight, dt_bias[None], a_log,
    )
    both = lax.all_gather(jnp.stack([decay, last]), "seq")
    start = ssm_state
    for k in range(7):
        start = jnp.where(k < s, both[k, 0] * start + both[k, 1], start)
    gated = call(
        scan_final,
        bf16(256, 512),
        [VMEM((16, 16, 128), jnp.float32), VMEM((4096, 512), jnp.bfloat16), VMEM((256, 512), jnp.float32)],
        bc, step, dtx, inner_u, z_inner, skip[None], a_log, start,
    )
    whole_out = lax.all_gather(out_weight, "seq", axis=1, tiled=True)
    return call_tail(
        gated, hidden, expert_ids, expert_gates, moe_gain[None], whole_out, expert_gate, expert_up, expert_down
    )


def solution(mesh):
    placed = (
        P("seq", "tp"),
        P("seq", None),
        P("seq", None),
        P(),
        P("seq", "tp"),
        P("seq", "tp"),
        P(None, "tp"),
        P("tp"),
        P("tp", None),
        P(None, "tp"),
        P("tp"),
        P(None, "tp"),
        P("tp"),
        P(None, "tp"),
        P("tp", "seq"),
        P(),
        P("seq", None, "tp"),
        P("seq", None, "tp"),
        P("seq", "tp", None),
    )
    return jax.shard_map(local, mesh=mesh, in_specs=placed, out_specs=P("seq", "tp"), check_vma=False)
```

```python
import jax
import jax.numpy as jnp
from jax import lax
from jax.experimental import pallas as pl
from jax.experimental.pallas import tpu as pltpu
from jax.sharding import PartitionSpec as P

EPS = 1e-06
LOG2E = 1.4426950408889634
VMEM = pltpu.VMEM


def softplus(v):
    return jnp.maximum(v, 0.0) + jnp.log1p(jnp.exp(-jnp.abs(v)))


def silu(v):
    return v / (1.0 + jnp.exp(-v))


def spread_b(bc, bt_ref):
    flipped = bc.T
    for g in range(16):
        bt_ref[g, :, 0:16] = flipped[0:16, 16 * g : 16 * g + 16]


def block_c(bc):
    row = lax.broadcasted_iota(jnp.int32, (128, 256), 0)
    col = lax.broadcasted_iota(jnp.int32, (128, 256), 1)
    tile = jnp.where(row - 16 == col % 16, 1.0, 0.0).astype(jnp.bfloat16)
    wide = jnp.dot(bc.astype(jnp.bfloat16), tile, preferred_element_type=jnp.float32)
    row = lax.broadcasted_iota(jnp.int32, (256, 256), 0)
    col = lax.broadcasted_iota(jnp.int32, (256, 256), 1)
    return jnp.where(row % 16 == col // 16, wide, 0.0).astype(jnp.bfloat16)


def run_states(step_ref, dtx_ref, bt_ref, rate, start, keep):
    def group(g, state):
        rows = pl.ds(pl.multiple_of(g * 16, 16), 16)
        step = step_ref[rows, :]
        dtx = dtx_ref[rows, :]
        b = bt_ref[g]
        for j in range(16):
            decay = jnp.exp2(step[j : j + 1, :] * rate)
            state = decay * state + b[:, j : j + 1] * dtx[j : j + 1, :]
            if keep is not None:
                keep[pl.ds(pl.multiple_of(g * 256 + 16 * j, 16), 16), :] = state.astype(jnp.bfloat16)
        return state

    return lax.fori_loop(0, 16, group, start)


def bf16(*shape):
    return jax.ShapeDtypeStruct(shape, jnp.bfloat16)


MESH = pl.DeviceIdType.MESH


def here():
    s, t = lax.axis_index("seq"), lax.axis_index("tp")
    return s, t, t // 4, t % 4


def remote(src, dst, sems, kind, device):
    return pltpu.make_async_remote_copy(
        src_ref=src,
        dst_ref=dst,
        send_sem=sems[0].at[kind],
        recv_sem=sems[1].at[kind],
        device_id=device,
        device_id_type=MESH,
    )


def slot_of(h, f, g):
    _, _, y, x = here()
    dy, dx = (g, f) if h == 0 else (f, g)
    return (y + dy) % 4 * 4 + (x + dx) % 4


def f_peer(h, d):
    return {"tp": slot_of(h, d, 0)}


def g_peer(h, d):
    return {"tp": slot_of(h, 0, d)}


def greet(seq_steps, tp_peers=None):
    s, _, _, _ = here()
    barrier = pltpu.get_barrier_semaphore()
    peers = [f_peer(0, 1), f_peer(0, 3), g_peer(0, 1), g_peer(0, 3)]
    if tp_peers is not None:
        peers = [{"tp": peer} for peer in tp_peers]
    peers += [{"seq": (s + d) % 8} for d in seq_steps]
    for peer in peers:
        pl.semaphore_signal(barrier, inc=1, device_id=peer, device_id_type=MESH)
    pl.semaphore_wait(barrier, len(peers))


def gather_tp(full, halves, sems, ready=lambda: None):
    def part(h, f, g, piece):
        lo, mid, hi = halves[h]
        a, b = {"h": (lo, hi), "q1": (lo, mid), "q2": (mid, hi)}[piece]
        return full.at[slot_of(h, f, g), a:b, :]

    def move(h, axis, f, piece, out, kind):
        d = 1 if kind in (0, 2) else 3
        if axis == "f":
            ref = part(h, out, 0, piece)
            return remote(ref, ref, (sems[0].at[h], sems[1].at[h]), 16 + kind, f_peer(h, d))
        ref = part(h, f, out, piece)
        return remote(ref, ref, (sems[0].at[h], sems[1].at[h]), f * 4 + kind, g_peer(h, d))

    def send(h, axis, f, kind):
        off = {0: 0, 1: 0, 2: 3, 3: 1}[kind]
        move(h, axis, f, {0: "h", 1: "h", 2: "q1", 3: "q2"}[kind], off, kind).start()

    def arrived(h, axis, f, kind):
        off = {0: 3, 1: 1, 2: 2, 3: 2}[kind]
        move(h, axis, f, {0: "h", 1: "h", 2: "q1", 3: "q2"}[kind], off, kind).wait_recv()

    def sent(h, axis, f, kind):
        off = {0: 0, 1: 0, 2: 3, 3: 1}[kind]
        move(h, axis, f, {0: "h", 1: "h", 2: "q1", 3: "q2"}[kind], off, kind).wait_send()

    def begin(h):
        for kind in (0, 1):
            send(h, "f", 0, kind)
        for kind in (0, 1):
            send(h, "g", 0, kind)

    def second(h):
        for kind, f in ((0, 3), (1, 1)):
            arrived(h, "f", 0, kind)
            send(h, "f", 0, kind + 2)
            send(h, "g", f, 0)
            send(h, "g", f, 1)

    def onward(h, f):
        for kind in (0, 1):
            arrived(h, "g", f, kind)
            send(h, "g", f, kind + 2)

    def third(h):
        for kind in (2, 3):
            arrived(h, "f", 0, kind)
        send(h, "g", 2, 0)
        send(h, "g", 2, 1)

    def last(h):
        for f in range(4):
            for kind in (2, 3):
                arrived(h, "g", f, kind)

    def finish():
        for h in (0, 1):
            for kind in range(4):
                sent(h, "f", 0, kind)
            for f in range(4):
                for kind in range(4):
                    sent(h, "g", f, kind)

    stages = [
        lambda: [begin(0), ready(), begin(1)],
        lambda: [second(h) for h in (0, 1)],
        lambda: [onward(h, 0) for h in (0, 1)],
        lambda: [third(h) for h in (0, 1)],
        lambda: [onward(h, f) for f in (3, 1) for h in (0, 1)],
        lambda: [onward(h, 2) for h in (0, 1)],
        lambda: [last(h) for h in (0, 1)],
    ]
    return stages, finish


def add_to(ref, *others):
    total = ref[...].astype(jnp.float32)
    for other in others:
        total = total + other[...].astype(jnp.float32)
    ref[...] = total.astype(jnp.bfloat16)


def scatter_tp(part, half, quarter, fill, bufs, sems):
    uq, uh, vq, vh = bufs

    def rows(h, piece):
        lo = h * half
        a, b = {"h": (lo, lo + half), "q1": (lo, lo + quarter), "q2": (lo + quarter, lo + half)}[piece]
        return slice(a, b)

    def spot(h, f, g, piece):
        return part.at[slot_of(h, f, g), rows(h, piece), :]

    names = ("q1", "q2", "h", "h")
    offs = (2, 2, 1, 3)

    def u_move(h, f, kind):
        dst = (uq.at[h, f, kind] if kind < 2 else uh.at[h, f, kind - 2])
        src = spot(h, f, offs[kind], names[kind])
        return remote(src, dst, (sems[0].at[h], sems[1].at[h]), f * 4 + kind, g_peer(h, 1 if kind % 2 == 0 else 3))

    def v_move(h, kind):
        dst = (vq.at[h, kind] if kind < 2 else vh.at[h, kind - 2])
        src = spot(h, offs[kind], 0, names[kind])
        return remote(src, dst, (sems[0].at[h], sems[1].at[h]), 16 + kind, f_peer(h, 1 if kind % 2 == 0 else 3))

    def each(fn):
        for h in (0, 1):
            lax.fori_loop(0, 4, lambda f, _, h=h: (fn(h, f), 0)[1], 0)

    def step1(h, f):
        fill(slot_of(h, f, 2), h)
        u_move(h, f, 0).start()
        u_move(h, f, 1).start()

    def made(h, f):
        fill(slot_of(h, f, 1), h)
        fill(slot_of(h, f, 3), h)

    def step2(h, f):
        for kind, g, piece in ((0, 1, "q1"), (1, 3, "q2")):
            u_move(h, f, kind).wait_recv()
            add_to(spot(h, f, g, piece), uq.at[h, f, kind])
            u_move(h, f, kind + 2).start()

    def own(h, f):
        fill(slot_of(h, f, 0), h)

    def step3(h, f):
        u_move(h, f, 2).wait_recv()
        u_move(h, f, 3).wait_recv()
        add_to(spot(h, f, 0, "h"), uh.at[h, f, 0], uh.at[h, f, 1])

    each(step1)
    each(made)
    each(step2)
    each(own)
    for h in (0, 1):
        step3(h, 2)
        v_move(h, 0).start()
        v_move(h, 1).start()
    for f, kind, piece in ((1, 0, "q1"), (3, 1, "q2")):
        for h in (0, 1):
            step3(h, f)
            v_move(h, kind).wait_recv()
            add_to(spot(h, f, 0, piece), vq.at[h, kind])
            v_move(h, kind + 2).start()
    for h in (0, 1):
        step3(h, 0)
    for h in (0, 1):
        v_move(h, 2).wait_recv()
        v_move(h, 3).wait_recv()
        add_to(spot(h, 0, 0, "h"), vh.at[h, 0], vh.at[h, 1])

    def finish():
        def u_sent(h, f):
            for kind in range(4):
                u_move(h, f, kind).wait_send()

        each(u_sent)
        for h in (0, 1):
            for kind in range(4):
                v_move(h, kind).wait_send()

    return finish


def tail(
    resid, ids, gates, gain, gate_hbm, up_hbm, down_hbm,
    out,
    gate_w, up_w, down_w, outgoing, full, normed, active, parts, back,
    pq, ph, pvq, pvh,
    w_sem, g_send, g_recv, p_send, p_recv, a_send, a_recv, b_send, b_recv,
):
    s, t, _, _ = here()
    loads = [
        pltpu.make_async_copy(src.at[0], dst, w_sem.at[i])
        for i, (src, dst) in enumerate(((gate_hbm, gate_w), (up_hbm, up_w), (down_hbm, down_w)))
    ]
    for load in loads:
        load.start()
    greet(range(1, 8))

    lane = lax.broadcasted_iota(jnp.int32, (256, 128), 1)
    either = jnp.where((lane == ids[:, 0:1]) | (lane == ids[:, 1:2]), 1.0, 0.0).astype(jnp.bfloat16)
    row = lax.broadcasted_iota(jnp.int32, (256, 256), 0)
    col = lax.broadcasted_iota(jnp.int32, (256, 256), 1)
    before = jnp.where(row > col, 1.0, 0.0).astype(jnp.bfloat16)
    slots = jnp.dot(before, either, preferred_element_type=jnp.float32)
    column = lax.broadcasted_iota(jnp.int32, (256, 768), 1).astype(jnp.float32)

    def pick(k):
        mine = ids[:, k : k + 1]
        place = jnp.sum(jnp.where(lane == mine, slots, 0.0), axis=1, keepdims=True)
        target = place + 96.0 * mine.astype(jnp.float32)
        return jnp.where(column == target, 1.0, 0.0).astype(jnp.bfloat16)

    outgoing[...] = lax.dot_general(
        pick(0) + pick(1), resid[...], (((0,), (0,)), ((), ())), preferred_element_type=jnp.float32
    ).astype(jnp.bfloat16)

    def mine(ref, k):
        return ref.at[pl.ds(pl.multiple_of(k * 96, 16), 96), :]

    def there(d):
        peer = (s + d) % 8
        return remote(mine(outgoing, peer), mine(full.at[t], s), (a_send, a_recv), d, {"seq": peer})

    for d in range(1, 8):
        there(d).start()
    full[t, pl.ds(pl.multiple_of(s * 96, 16), 96), :] = mine(outgoing, s)[...]
    for d in range(1, 8):
        there(d).wait_recv()

    stages, gathered = gather_tp(full, ((0, 192, 384), (384, 576, 768)), (g_send, g_recv))
    for stage in stages:
        stage()

    def squares(k, total):
        wide = full[k].astype(jnp.float32)
        return total + jnp.sum(wide * wide, axis=1, keepdims=True)

    total = lax.fori_loop(0, 16, squares, jnp.zeros((768, 1), jnp.float32))
    scale = lax.rsqrt(total * (1.0 / 4096.0) + EPS)

    def norm(k, _):
        cols = pl.ds(pl.multiple_of(k * 256, 256), 256)
        normed[:, cols] = (full[k].astype(jnp.float32) * scale * gain[:, cols]).astype(jnp.bfloat16)
        return 0

    lax.fori_loop(0, 16, norm, 0)
    loads[0].wait()
    loads[1].wait()

    def hidden_units(i, _):
        rows = pl.ds(pl.multiple_of(i * 256, 256), 256)
        for j in range(3):
            cols = slice(j * 256, j * 256 + 256)
            a = jnp.dot(normed[rows, :], gate_w[:, cols], preferred_element_type=jnp.float32)
            b = jnp.dot(normed[rows, :], up_w[:, cols], preferred_element_type=jnp.float32)
            active[rows, cols] = (silu(a) * b).astype(jnp.bfloat16)
        return 0

    lax.fori_loop(0, 3, hidden_units, 0)
    loads[2].wait()

    def fill_parts(slot, h):
        cols = pl.ds(pl.multiple_of(slot * 256, 256), 256)
        parts[slot, h * 384 : h * 384 + 384, :] = jnp.dot(
            active[h * 384 : h * 384 + 384, :], down_w[:, cols], preferred_element_type=jnp.float32
        ).astype(jnp.bfloat16)

    parts_done = scatter_tp(parts, 384, 192, fill_parts, (pq, ph, pvq, pvh), (p_send, p_recv))

    def home(d):
        peer = (s + d) % 8
        return remote(mine(parts.at[t], peer), mine(back, s), (b_send, b_recv), d, {"seq": peer})

    for d in range(1, 8):
        home(d).start()
    mine(back, s)[...] = mine(parts.at[t], s)[...]
    for d in range(1, 8):
        home(d).wait_recv()
    total = resid[...].astype(jnp.float32)
    for k in range(2):
        total = total + gates[:, k : k + 1] * jnp.dot(pick(k), back[...], preferred_element_type=jnp.float32)
    out[...] = total.astype(jnp.bfloat16)

    gathered()
    parts_done()
    for d in range(1, 8):
        there(d).wait_send()
        home(d).wait_send()


def sum_bufs(half):
    b16, q = jnp.bfloat16, half // 2
    return [
        VMEM((2, 4, 2, q, 256), b16), VMEM((2, 4, 2, half, 256), b16), VMEM((2, 2, q, 256), b16), VMEM((2, 2, half, 256), b16)
    ]


def call_tail(*args):
    vm, hbm = pl.BlockSpec(memory_space=pltpu.VMEM), pl.BlockSpec(memory_space=pl.ANY)
    b16 = jnp.bfloat16
    dma = pltpu.SemaphoreType.DMA
    return pl.pallas_call(
        tail,
        out_shape=bf16(256, 256),
        in_specs=[vm] * 4 + [hbm] * 3,
        out_specs=vm,
        scratch_shapes=[
            VMEM((4096, 768), b16), VMEM((4096, 768), b16), VMEM((768, 4096), b16),
            VMEM((768, 256), b16), VMEM((16, 768, 256), b16), VMEM((768, 4096), b16),
            VMEM((768, 768), b16), VMEM((16, 768, 256), b16), VMEM((768, 256), b16),
            *sum_bufs(384),
            dma((3,)), dma((2, 20)), dma((2, 20)), dma((2, 20)), dma((2, 20)),
            dma((8,)), dma((8,)), dma((8,)), dma((8,)),
        ],
        compiler_params=pltpu.CompilerParams(collective_id=1, has_side_effects=True, vmem_limit_bytes=60 << 20),
    )(*args)


def gather_seq(own, full, sems):
    s, _, _, _ = here()
    z, core = s // 2, s % 2

    def slot(dz, other=0):
        return (z + dz) % 4 * 2 + (core + other) % 2

    rows = {"q1": slice(0, 256), "q2": slice(256, 512), "all": slice(0, 512)}
    plan = [
        (0, "q1", 1), (0, "q2", 3), (0, "q2", 1), (0, "q1", 3), (3, "q1", 1), (1, "q2", 3),
        (0, "all", 0), (3, "all", 0), (1, "all", 0), (2, "q1", 0), (2, "q2", 0),
    ]

    def copy(kind, arriving):
        dz, piece, step = plan[kind]
        k = slot((dz - step) % 4, 0 if step else 1) if arriving else slot(dz)
        dst = full.at[k, rows[piece], :]
        src = own.at[rows[piece], :] if dz == 0 and not arriving else dst
        peer = slot(step) if step else slot(0, 1)
        return remote(src, dst, sems, kind, {"seq": peer})

    def send(*kinds):
        for kind in kinds:
            copy(kind, False).start()

    def wait(*kinds):
        for kind in kinds:
            copy(kind, True).wait_recv()

    def finish():
        for kind in range(11):
            copy(kind, False).wait_send()

    return slot, send, wait, finish


def head(
    hidden, gain, conv_w, conv_b, x_proj, dt_w, dt_b, a_log, skip, ssm_state, in_x, in_z, out_w,
    resid,
    wx, wz, wo, full, normed, xs, zs, u, share, heard, proj, step, dtx, bt, kept, y, states, gated, terms,
    tq, th, tvq, tvh,
    l_sem, h_sem, w_send, w_recv, g_send, g_recv, r_send, r_recv, c_send, c_recv, s_send, s_recv, t_send, t_recv,
):
    s, t, _, _ = here()
    loads = [
        pltpu.make_async_copy(src, dst.at[s], l_sem.at[i]) for i, (src, dst) in enumerate(((in_x, wx), (in_z, wz), (out_w, wo)))
    ]
    for load in loads:
        load.start()
    full[t, 16:272, :] = hidden[...]
    greet(range(1, 8), [(t + d) % 16 for d in range(1, 16)])

    slot, x_send, x_wait, x_done = gather_seq(in_x, wx, (w_send.at[0], w_recv.at[0]))
    _, z_send, z_wait, z_done = gather_seq(in_z, wz, (w_send.at[1], w_recv.at[1]))
    _, o_send, o_wait, o_done = gather_seq(out_w, wo, (w_send.at[2], w_recv.at[2]))

    halo = remote(hidden.at[240:256, :], full.at[t, 0:16, :], (h_sem.at[0], h_sem.at[1]), 0, {"seq": (s + 1) % 8})
    halo.start()
    x_send(0, 1, 2, 3)
    stages, gathered = gather_tp(full, ((144, 208, 272), (0, 80, 144)), (g_send, g_recv), halo.wait_recv)
    stages[0]()
    x_send(6)
    for stage in stages[1:4]:
        stage()
    x_wait(0)
    x_send(4)
    x_wait(1)
    x_send(5)
    for stage in stages[4:]:
        stage()

    def squares(k, total):
        wide = full[k].astype(jnp.float32)
        return total + jnp.sum(wide * wide, axis=1, keepdims=True)

    total = lax.fori_loop(0, 16, squares, jnp.zeros((272, 1), jnp.float32))
    scale = lax.rsqrt(total * (1.0 / 4096.0) + EPS)

    def norm(k, _):
        cols = pl.ds(pl.multiple_of(k * 256, 256), 256)
        normed[:, cols] = (full[k].astype(jnp.float32) * scale * gain[:, cols]).astype(jnp.bfloat16)
        return 0

    lax.fori_loop(0, 16, norm, 0)

    def product(total, first, weight, k):
        cols = pl.ds(pl.multiple_of(k * 512, 512), 512)
        term = jnp.dot(normed[first:272, cols], weight[k], preferred_element_type=jnp.float32)
        total[...] = total[...] + term

    xs[...] = jnp.zeros_like(xs)
    loads[0].wait()
    product(xs, 0, wx, slot(0))
    x_wait(2, 3)
    x_send(7, 8)
    product(xs, 0, wx, slot(3))
    product(xs, 0, wx, slot(1))
    x_wait(4, 5)
    x_send(9, 10)
    z_send(0, 1, 2, 3, 6)
    product(xs, 0, wx, slot(2))
    x_wait(6, 7, 8)
    for dz in (0, 3, 1):
        product(xs, 0, wx, slot(dz, 1))
    x_wait(9, 10)
    product(xs, 0, wx, slot(2, 1))

    xs[...] = xs[...].astype(jnp.bfloat16).astype(jnp.float32)
    xs[0:16, :] = jnp.where(s > 0, xs[0:16, :], 0.0)
    total = conv_b[...]
    for tap in range(4):
        total = total + conv_w[tap : tap + 1, :] * xs[13 + tap : 269 + tap, :]
    u[...] = silu(total).astype(jnp.bfloat16)

    low = jnp.dot(u[...], x_proj[:, 0:512], preferred_element_type=jnp.float32).astype(jnp.bfloat16)
    rest = jnp.dot(u[...], x_proj[:, 512:544], preferred_element_type=jnp.float32).astype(jnp.bfloat16)
    rest = jnp.concatenate([rest, jnp.zeros((256, 96), jnp.bfloat16)], axis=1)
    for g in range(16):
        share[g, :, 0:512] = low[16 * g : 16 * g + 16, :]
        share[g, :, 512:640] = rest[16 * g : 16 * g + 16, :]

    def give(d, arriving=False):
        peer = (t + d) % 16
        k = (t + 16 - d) % 16 if arriving else t
        return remote(share.at[peer], heard.at[k], (r_send, r_recv), d, {"tp": peer})

    def tell(d, arriving=False):
        peer = (t + d) % 16
        k = (t + 16 - d) % 16 if arriving else t
        return remote(proj.at[k], proj.at[k], (c_send, c_recv), d, {"tp": peer})

    def others(fn, count=16):
        lax.fori_loop(1, count, lambda d, _: (fn(d), 0)[1], 0)

    others(lambda d: give(d).start())
    heard[t] = share[t]
    others(lambda d: give(d, True).wait_recv())
    proj[t] = lax.fori_loop(
        0, 16, lambda k, total: total + heard[k].astype(jnp.float32), jnp.zeros((16, 640), jnp.float32)
    ).astype(jnp.bfloat16)
    others(lambda d: tell(d).start())
    z_wait(0)
    z_send(4)
    z_wait(1)
    z_send(5)
    others(lambda d: tell(d, True).wait_recv())

    low = proj[:, :, 0:512].reshape(256, 512)
    bc = proj[:, :, 512:640].reshape(256, 128).astype(jnp.float32)
    size = softplus(jnp.dot(low, dt_w[...], preferred_element_type=jnp.float32) + dt_b[...])
    step[...] = size
    dtx[...] = size * u[...].astype(jnp.float32)
    spread_b(bc, bt)
    rate = jnp.exp(a_log[...]) * (-LOG2E)
    states[s, 0:16, :] = jnp.exp2(rate * jnp.sum(size, axis=0, keepdims=True)).astype(jnp.bfloat16)
    states[s, 16:32, :] = run_states(step, dtx, bt, rate, jnp.zeros((16, 512), jnp.float32), None).astype(jnp.bfloat16)

    def pass_on(d, arriving=False):
        k = (s + 8 - d) % 8 if arriving else s
        return remote(states.at[k], states.at[k], (s_send, s_recv), d, {"seq": (s + d) % 8})

    lax.fori_loop(1, 8 - s, lambda d, _: (pass_on(d).start(), 0)[1], 0)
    z_wait(2, 3)
    z_send(7, 8)
    o_send(0, 1, 2, 3, 6)
    zs[...] = jnp.zeros_like(zs)
    loads[1].wait()
    for dz in (0, 3, 1):
        product(zs, 16, wz, slot(dz))
    z_wait(4, 5)
    z_send(9, 10)
    lax.fori_loop(1, s + 1, lambda d, _: (pass_on(d, True).wait_recv(), 0)[1], 0)

    def enter(k, state):
        return states[k, 0:16, :].astype(jnp.float32) * state + states[k, 16:32, :].astype(jnp.float32)

    start = lax.fori_loop(0, s, enter, ssm_state[...])
    run_states(step, dtx, bt, rate, start, kept)
    o_wait(0)
    o_send(4)
    o_wait(1)
    o_send(5)
    c = block_c(bc)
    for g in range(16):
        y[16 * g : 16 * g + 16, :] = jnp.dot(
            c[16 * g : 16 * g + 16, :], kept[256 * g : 256 * g + 256, :], preferred_element_type=jnp.float32
        )
    z_wait(6, 7, 8, 9, 10)
    product(zs, 16, wz, slot(2))
    for dz in range(4):
        product(zs, 16, wz, slot(dz, 1))
    gate = silu(zs[...].astype(jnp.bfloat16).astype(jnp.float32))
    gated[...] = ((y[...] + skip[...] * u[...].astype(jnp.float32)) * gate).astype(jnp.bfloat16)
    o_wait(2, 3)
    o_send(7, 8)
    loads[2].wait()
    o_wait(4, 5)
    o_send(9, 10)
    o_wait(6, 7, 8, 9, 10)

    def fill_terms(k, h):
        cols = pl.ds(pl.multiple_of(k % 2 * 256, 256), 256)
        terms[k, h * 128 : h * 128 + 128, :] = jnp.dot(
            gated[h * 128 : h * 128 + 128, :], wo[k // 2, :, cols], preferred_element_type=jnp.float32
        ).astype(jnp.bfloat16)

    terms_done = scatter_tp(terms, 128, 64, fill_terms, (tq, th, tvq, tvh), (t_send, t_recv))
    resid[...] = (hidden[...].astype(jnp.float32) + terms[t].astype(jnp.float32)).astype(jnp.bfloat16)

    halo.wait_send()
    gathered()
    x_done()
    z_done()
    o_done()
    others(lambda d: give(d).wait_send())
    others(lambda d: tell(d).wait_send())
    lax.fori_loop(1, 8 - s, lambda d, _: (pass_on(d).wait_send(), 0)[1], 0)
    terms_done()


def call_head(*args):
    vm, hbm = pl.BlockSpec(memory_space=pltpu.VMEM), pl.BlockSpec(memory_space=pl.ANY)
    b16, wide = jnp.bfloat16, jnp.float32
    dma = pltpu.SemaphoreType.DMA
    return pl.pallas_call(
        head,
        out_shape=bf16(256, 256),
        in_specs=[vm] * 10 + [hbm] * 3,
        out_specs=vm,
        scratch_shapes=[
            VMEM((8, 512, 512), b16), VMEM((8, 512, 512), b16), VMEM((8, 512, 512), b16),
            VMEM((16, 272, 256), b16), VMEM((272, 4096), b16), VMEM((272, 512), wide), VMEM((256, 512), wide),
            VMEM((256, 512), b16), VMEM((16, 16, 640), b16), VMEM((16, 16, 640), b16), VMEM((16, 16, 640), b16),
            VMEM((256, 512), wide), VMEM((256, 512), wide), VMEM((16, 16, 128), wide), VMEM((4096, 512), b16),
            VMEM((256, 512), wide), VMEM((8, 32, 512), b16), VMEM((256, 512), b16), VMEM((16, 256, 256), b16),
            *sum_bufs(128),
            dma((3,)), dma((2, 1)), dma((3, 11)), dma((3, 11)), dma((2, 20)), dma((2, 20)), dma((16,)), dma((16,)),
            dma((16,)), dma((16,)), dma((8,)), dma((8,)), dma((2, 20)), dma((2, 20)),
        ],
        compiler_params=pltpu.CompilerParams(collective_id=2, has_side_effects=True, vmem_limit_bytes=60 << 20),
    )(*args)


def local(
    hidden,
    expert_ids,
    expert_gates,
    mamba_gain,
    in_x_weight,
    in_z_weight,
    conv_weight,
    conv_bias,
    x_proj_weight,
    dt_weight,
    dt_bias,
    a_log,
    skip,
    ssm_state,
    out_weight,
    moe_gain,
    expert_gate,
    expert_up,
    expert_down,
):
    residual = call_head(
        hidden, mamba_gain[None], conv_weight, conv_bias[None], x_proj_weight, dt_weight, dt_bias[None], a_log, skip[None],
        ssm_state, in_x_weight, in_z_weight, out_weight,
    )
    return call_tail(residual, expert_ids, expert_gates, moe_gain[None], expert_gate, expert_up, expert_down)


def solution(mesh):
    placed = (
        P("seq", "tp"),
        P("seq", None),
        P("seq", None),
        P(),
        P("seq", "tp"),
        P("seq", "tp"),
        P(None, "tp"),
        P("tp"),
        P("tp", None),
        P(None, "tp"),
        P("tp"),
        P(None, "tp"),
        P("tp"),
        P(None, "tp"),
        P("tp", "seq"),
        P(),
        P("seq", None, "tp"),
        P("seq", None, "tp"),
        P("seq", "tp", None),
    )
    return jax.shard_map(local, mesh=mesh, in_specs=placed, out_specs=P("seq", "tp"), check_vma=False)
```

```python
import jax
import jax.numpy as jnp
from jax import lax
from jax.experimental import pallas as pl
from jax.experimental.pallas import tpu as pltpu
from jax.sharding import PartitionSpec as P

EPS = 1e-06
LOG2E = 1.4426950408889634
VMEM = pltpu.VMEM


def softplus(v):
    return jnp.maximum(v, 0.0) + jnp.log1p(jnp.exp(-jnp.abs(v)))


def silu(v):
    return v / (1.0 + jnp.exp(-v))


def spread_b(bc, bt_ref):
    flipped = bc.T
    for g in range(16):
        bt_ref[g, :, 0:16] = flipped[0:16, 16 * g : 16 * g + 16]


def block_c(bc):
    row = lax.broadcasted_iota(jnp.int32, (128, 256), 0)
    col = lax.broadcasted_iota(jnp.int32, (128, 256), 1)
    tile = jnp.where(row - 16 == col % 16, 1.0, 0.0).astype(jnp.bfloat16)
    wide = jnp.dot(bc.astype(jnp.bfloat16), tile, preferred_element_type=jnp.float32)
    row = lax.broadcasted_iota(jnp.int32, (256, 256), 0)
    col = lax.broadcasted_iota(jnp.int32, (256, 256), 1)
    return jnp.where(row % 16 == col // 16, wide, 0.0).astype(jnp.bfloat16)


def run_states(step_ref, dtx_ref, bt_ref, rate, start, keep):
    def group(g, state):
        rows = pl.ds(pl.multiple_of(g * 16, 16), 16)
        step = step_ref[rows, :]
        dtx = dtx_ref[rows, :]
        b = bt_ref[g]
        for j in range(16):
            decay = jnp.exp2(step[j : j + 1, :] * rate)
            state = decay * state + b[:, j : j + 1] * dtx[j : j + 1, :]
            if keep is not None:
                keep[pl.ds(pl.multiple_of(g * 256 + 16 * j, 16), 16), :] = state.astype(jnp.bfloat16)
        return state

    return lax.fori_loop(0, 16, group, start)


def bf16(*shape):
    return jax.ShapeDtypeStruct(shape, jnp.bfloat16)


MESH = pl.DeviceIdType.MESH


def here():
    s, t = lax.axis_index("seq"), lax.axis_index("tp")
    return s, t, t // 4, t % 4


def remote(src, dst, sems, kind, device):
    return pltpu.make_async_remote_copy(
        src_ref=src,
        dst_ref=dst,
        send_sem=sems[0].at[kind],
        recv_sem=sems[1].at[kind],
        device_id=device,
        device_id_type=MESH,
    )


def slot_of(h, f, g):
    _, _, y, x = here()
    dy, dx = (g, f) if h == 0 else (f, g)
    return (y + dy) % 4 * 4 + (x + dx) % 4


def f_peer(h, d):
    return {"tp": slot_of(h, d, 0)}


def g_peer(h, d):
    return {"tp": slot_of(h, 0, d)}


def greet(seq_steps, tp_peers=None):
    s, _, _, _ = here()
    barrier = pltpu.get_barrier_semaphore()
    peers = [f_peer(0, 1), f_peer(0, 3), g_peer(0, 1), g_peer(0, 3)]
    if tp_peers is not None:
        peers = [{"tp": peer} for peer in tp_peers]
    peers += [{"seq": (s + d) % 8} for d in seq_steps]
    for peer in peers:
        pl.semaphore_signal(barrier, inc=1, device_id=peer, device_id_type=MESH)
    pl.semaphore_wait(barrier, len(peers))


def gather_tp(full, halves, sems, ready=lambda: None):
    def part(h, f, g, piece):
        lo, mid, hi = halves[h]
        a, b = {"h": (lo, hi), "q1": (lo, mid), "q2": (mid, hi)}[piece]
        return full.at[slot_of(h, f, g), a:b, :]

    def move(h, axis, f, piece, out, kind):
        d = 1 if kind in (0, 2) else 3
        if axis == "f":
            ref = part(h, out, 0, piece)
            return remote(ref, ref, (sems[0].at[h], sems[1].at[h]), 16 + kind, f_peer(h, d))
        ref = part(h, f, out, piece)
        return remote(ref, ref, (sems[0].at[h], sems[1].at[h]), f * 4 + kind, g_peer(h, d))

    def send(h, axis, f, kind):
        off = {0: 0, 1: 0, 2: 3, 3: 1}[kind]
        move(h, axis, f, {0: "h", 1: "h", 2: "q1", 3: "q2"}[kind], off, kind).start()

    def arrived(h, axis, f, kind):
        off = {0: 3, 1: 1, 2: 2, 3: 2}[kind]
        move(h, axis, f, {0: "h", 1: "h", 2: "q1", 3: "q2"}[kind], off, kind).wait_recv()

    def sent(h, axis, f, kind):
        off = {0: 0, 1: 0, 2: 3, 3: 1}[kind]
        move(h, axis, f, {0: "h", 1: "h", 2: "q1", 3: "q2"}[kind], off, kind).wait_send()

    def begin(h):
        for kind in (0, 1):
            send(h, "f", 0, kind)
        for kind in (0, 1):
            send(h, "g", 0, kind)

    def second(h):
        for kind, f in ((0, 3), (1, 1)):
            arrived(h, "f", 0, kind)
            send(h, "f", 0, kind + 2)
            send(h, "g", f, 0)
            send(h, "g", f, 1)

    def onward(h, f):
        for kind in (0, 1):
            arrived(h, "g", f, kind)
            send(h, "g", f, kind + 2)

    def third(h):
        for kind in (2, 3):
            arrived(h, "f", 0, kind)
        send(h, "g", 2, 0)
        send(h, "g", 2, 1)

    def last(h):
        for f in range(4):
            for kind in (2, 3):
                arrived(h, "g", f, kind)

    def finish():
        for h in (0, 1):
            for kind in range(4):
                sent(h, "f", 0, kind)
            for f in range(4):
                for kind in range(4):
                    sent(h, "g", f, kind)

    stages = [
        lambda: [begin(0), ready(), begin(1)],
        lambda: [second(h) for h in (0, 1)],
        lambda: [onward(h, 0) for h in (0, 1)],
        lambda: [third(h) for h in (0, 1)],
        lambda: [onward(h, f) for f in (3, 1) for h in (0, 1)],
        lambda: [onward(h, 2) for h in (0, 1)],
        lambda: [last(h) for h in (0, 1)],
    ]
    return stages, finish


def add_to(ref, *others):
    total = ref[...].astype(jnp.float32)
    for other in others:
        total = total + other[...].astype(jnp.float32)
    ref[...] = total.astype(jnp.bfloat16)


def scatter_tp(part, first, half, fill, bufs, sems):
    uq, uh, vq, vh = bufs
    quarter = half // 2

    def rows(h, piece):
        lo = first + h * half
        a, b = {"h": (lo, lo + half), "q1": (lo, lo + quarter), "q2": (lo + quarter, lo + half)}[piece]
        return slice(a, b)

    def spot(h, f, g, piece):
        return part.at[slot_of(h, f, g), rows(h, piece), :]

    names = ("q1", "q2", "h", "h")
    offs = (2, 2, 1, 3)

    def u_move(h, f, kind):
        dst = uq.at[h, f, kind] if kind < 2 else uh.at[h, f, kind - 2]
        src = spot(h, f, offs[kind], names[kind])
        return remote(src, dst, (sems[0].at[h], sems[1].at[h]), f * 4 + kind, g_peer(h, 1 if kind % 2 == 0 else 3))

    def v_move(h, kind):
        dst = vq.at[h, kind] if kind < 2 else vh.at[h, kind - 2]
        src = spot(h, offs[kind], 0, names[kind])
        return remote(src, dst, (sems[0].at[h], sems[1].at[h]), 16 + kind, f_peer(h, 1 if kind % 2 == 0 else 3))

    def each(fn):
        for h in (0, 1):
            lax.fori_loop(0, 4, lambda f, _, h=h: (fn(h, f), 0)[1], 0)

    def step1():
        def far_rows(f, _):
            fill(slot_of(0, f, 2))
            u_move(0, f, 0).start()
            u_move(0, f, 1).start()
            return 0

        lax.fori_loop(0, 4, far_rows, 0)
        for f in (2, 0, 1, 3):
            if f != 2:
                fill(slot_of(1, f, 2))
            u_move(1, f, 0).start()
            u_move(1, f, 1).start()

    def made():
        def near(i, _):
            f, g = i // 3 + i // 6, i % 3 + i % 3 // 2
            fill(slot_of(0, f, g))
            return 0

        lax.fori_loop(0, 9, near, 0)

    def pass_on(h, f):
        for kind, g, piece in ((0, 1, "q1"), (1, 3, "q2")):
            u_move(h, f, kind).wait_recv()
            add_to(spot(h, f, g, piece), uq.at[h, f, kind])
            u_move(h, f, kind + 2).start()

    def summed(h, f):
        u_move(h, f, 2).wait_recv()
        u_move(h, f, 3).wait_recv()
        add_to(spot(h, f, 0, "h"), uh.at[h, f, 0], uh.at[h, f, 1])

    def far():
        for h in (0, 1):
            summed(h, 2)
            v_move(h, 0).start()
            v_move(h, 1).start()

    def sides():
        for f, kind, piece in ((1, 0, "q1"), (3, 1, "q2")):
            for h in (0, 1):
                summed(h, f)
                v_move(h, kind).wait_recv()
                add_to(spot(h, f, 0, piece), vq.at[h, kind])
                v_move(h, kind + 2).start()

    def own():
        for h in (0, 1):
            summed(h, 0)

    def last():
        for h in (0, 1):
            v_move(h, 2).wait_recv()
            v_move(h, 3).wait_recv()
            add_to(spot(h, 0, 0, "h"), vh.at[h, 0], vh.at[h, 1])

    def finish():
        def u_sent(h, f):
            for kind in range(4):
                u_move(h, f, kind).wait_send()

        each(u_sent)
        for h in (0, 1):
            for kind in range(4):
                v_move(h, kind).wait_send()

    return [step1, made, lambda: each(pass_on), far, sides, own, last], finish


ORDER = (0, 1, 7, 2, 6, 3, 5, 4)


def tail(
    resid, ids, gates, gain, gate_hbm, up_hbm, down_hbm,
    out,
    gate_w, up_w, down_w, outgoing, full, normed, active, parts, back, places,
    pq, ph, pvq, pvh, rq, rh, rvq, rvh,
    w_sem, g_send, g_recv, p_send, p_recv, a_send, a_recv, b_send, b_recv,
):
    s, t, _, _ = here()
    loads = [
        pltpu.make_async_copy(src.at[0], dst, w_sem.at[i])
        for i, (src, dst) in enumerate(((gate_hbm, gate_w), (up_hbm, up_w), (down_hbm, down_w)))
    ]
    for load in loads:
        load.start()

    name = lax.broadcasted_iota(jnp.int32, (16, 256), 0)
    either = jnp.where((name == ids[0:1, :]) | (name == ids[1:2, :]), 1.0, 0.0).astype(jnp.bfloat16)
    row = lax.broadcasted_iota(jnp.int32, (256, 256), 0)
    col = lax.broadcasted_iota(jnp.int32, (256, 256), 1)
    before = jnp.where(row < col, 1.0, 0.0).astype(jnp.bfloat16)
    slots = jnp.dot(either, before, preferred_element_type=jnp.float32)
    line = lax.broadcasted_iota(jnp.int32, (768, 256), 0).astype(jnp.float32)

    def place(k):
        mine = ids[k : k + 1, :]
        target = jnp.sum(jnp.where(name == mine, slots, 0.0), axis=0, keepdims=True) + 96.0 * mine.astype(jnp.float32)
        return jnp.where(line == target, 1.0, 0.0)

    places[0] = place(0).astype(jnp.bfloat16)
    places[1] = place(1).astype(jnp.bfloat16)
    outgoing[...] = jnp.dot(places[0] + places[1], resid[...], preferred_element_type=jnp.float32).astype(jnp.bfloat16)
    greet(range(1, 8))

    def mine(ref, k):
        return ref.at[pl.ds(pl.multiple_of(k * 96, 16), 96), :]

    def there(i):
        d = ORDER[i]
        peer = (s + d) % 8
        return remote(mine(outgoing, peer), mine(full.at[t], i), (a_send, a_recv), i, {"seq": peer})

    for i in range(1, 8):
        there(i).start()
    full[t, 0:96, :] = mine(outgoing, s)[...]

    spread, spread_done = zip(
        *[
            gather_tp(
                full,
                ((c * 384, c * 384 + 96, c * 384 + 192), (c * 384 + 192, c * 384 + 288, c * 384 + 384)),
                (g_send.at[c], g_recv.at[c]),
            )
            for c in (0, 1)
        ]
    )

    def norm(c):
        rows = slice(c * 384, c * 384 + 384)

        def squares(k, total):
            wide = full[k, rows, :].astype(jnp.float32)
            wide = wide * wide
            return total + (wide[:, 0:128] + wide[:, 128:256])

        total = lax.fori_loop(0, 16, squares, jnp.zeros((384, 128), jnp.float32))
        scale = lax.rsqrt(jnp.sum(total, axis=1, keepdims=True) * (1.0 / 4096.0) + EPS)

        def apply(k, _):
            cols = pl.ds(pl.multiple_of(k * 256, 256), 256)
            normed[rows, cols] = (full[k, rows, :].astype(jnp.float32) * scale * gain[:, cols]).astype(jnp.bfloat16)
            return 0

        lax.fori_loop(0, 16, apply, 0)

    def hidden_units(c, j):
        rows, cols = slice(c * 384, c * 384 + 384), slice(j * 256, j * 256 + 256)
        a = jnp.dot(normed[rows, :], gate_w[:, cols], preferred_element_type=jnp.float32)
        b = jnp.dot(normed[rows, :], up_w[:, cols], preferred_element_type=jnp.float32)
        active[rows, cols] = (silu(a) * b).astype(jnp.bfloat16)

    def fill_parts(c):
        rows = slice(c * 384, c * 384 + 384)

        def fill(slot):
            cols = pl.ds(pl.multiple_of(slot * 256, 256), 256)
            parts[slot, rows, :] = jnp.dot(
                active[rows, :], down_w[:, cols], preferred_element_type=jnp.float32
            ).astype(jnp.bfloat16)

        return fill

    bufs = ((pq, ph, pvq, pvh), (rq, rh, rvq, rvh))
    total, total_done = zip(
        *[scatter_tp(parts, c * 384, 192, fill_parts(c), bufs[c], (p_send.at[c], p_recv.at[c])) for c in (0, 1)]
    )

    def home(i):
        peer = (s + 8 - ORDER[i]) % 8
        return remote(mine(parts.at[t], i), mine(back, s), (b_send, b_recv), i, {"seq": peer})

    def run(stages, *which):
        for i in which:
            stages[i]()

    for i in (1, 2, 3):
        there(i).wait_recv()
    run(spread[0], 0, 1)
    for i in (4, 5, 6, 7):
        there(i).wait_recv()
    run(spread[1], 0)
    run(spread[0], 2, 3)
    run(spread[1], 1)
    run(spread[0], 4)
    run(spread[1], 2)
    run(spread[0], 5)
    run(spread[1], 3)
    run(spread[0], 6)
    norm(0)
    run(spread[1], 4)
    loads[0].wait()
    loads[1].wait()
    hidden_units(0, 0)
    run(spread[1], 5)
    hidden_units(0, 1)
    hidden_units(0, 2)
    loads[2].wait()
    run(total[0], 0)
    run(spread[1], 6)
    run(total[0], 1, 2)
    norm(1)
    hidden_units(1, 0)
    run(total[0], 3)
    hidden_units(1, 1)
    run(total[0], 4)
    hidden_units(1, 2)
    run(total[1], 0)
    run(total[0], 5, 6)
    for i in (1, 2, 3):
        home(i).start()
    mine(back, s)[...] = parts[t, 0:96, :]
    run(total[1], 1, 2, 3, 4, 5, 6)
    for i in (4, 5, 6, 7):
        home(i).start()
    fine = [gates[k : k + 1, :] for k in (0, 1)]
    high = [g.astype(jnp.bfloat16).astype(jnp.float32) for g in fine]
    result = resid[...].astype(jnp.float32)
    wide = [places[k].astype(jnp.float32) for k in (0, 1)]
    weigh = [
        (wide[0] * g[0] + wide[1] * g[1]).astype(jnp.bfloat16) for g in (high, [fine[k] - high[k] for k in (0, 1)])
    ]
    for i in range(1, 8):
        home(i).wait_recv()
    for w in weigh:
        result = result + lax.dot_general(
            w, back[...], (((0,), (0,)), ((), ())), preferred_element_type=jnp.float32
        )
    out[...] = result.astype(jnp.bfloat16)

    for c in (0, 1):
        spread_done[c]()
        total_done[c]()
    for i in range(1, 8):
        there(i).wait_send()
        home(i).wait_send()


def sum_bufs(half):
    b16, q = jnp.bfloat16, half // 2
    return [
        VMEM((2, 4, 2, q, 256), b16), VMEM((2, 4, 2, half, 256), b16), VMEM((2, 2, q, 256), b16), VMEM((2, 2, half, 256), b16)
    ]


def call_tail(*args):
    vm, hbm = pl.BlockSpec(memory_space=pltpu.VMEM), pl.BlockSpec(memory_space=pl.ANY)
    b16 = jnp.bfloat16
    dma = pltpu.SemaphoreType.DMA
    return pl.pallas_call(
        tail,
        out_shape=bf16(256, 256),
        in_specs=[vm] * 4 + [hbm] * 3,
        out_specs=vm,
        scratch_shapes=[
            VMEM((4096, 768), b16), VMEM((4096, 768), b16), VMEM((768, 4096), b16),
            VMEM((768, 256), b16), VMEM((16, 768, 256), b16), VMEM((768, 4096), b16),
            VMEM((768, 768), b16), VMEM((16, 768, 256), b16), VMEM((768, 256), b16), VMEM((2, 768, 256), b16),
            *sum_bufs(192), *sum_bufs(192),
            dma((3,)), dma((2, 2, 20)), dma((2, 2, 20)), dma((2, 2, 20)), dma((2, 2, 20)),
            dma((8,)), dma((8,)), dma((8,)), dma((8,)),
        ],
        compiler_params=pltpu.CompilerParams(collective_id=1, has_side_effects=True, vmem_limit_bytes=60 << 20),
    )(*args)


def gather_seq(own, full, sems):
    s, _, _, _ = here()
    z, core = s // 2, s % 2

    def slot(dz, other=0):
        return (z + dz) % 4 * 2 + (core + other) % 2

    rows = {"q1": slice(0, 256), "q2": slice(256, 512), "all": slice(0, 512)}
    plan = [
        (0, "q1", 1), (0, "q2", 3), (0, "q2", 1), (0, "q1", 3), (3, "q1", 1), (1, "q2", 3),
        (0, "all", 0), (3, "all", 0), (1, "all", 0), (2, "q1", 0), (2, "q2", 0),
    ]

    def copy(kind, arriving):
        dz, piece, step = plan[kind]
        k = slot((dz - step) % 4, 0 if step else 1) if arriving else slot(dz)
        dst = full.at[k, rows[piece], :]
        src = own.at[rows[piece], :] if dz == 0 and not arriving else dst
        peer = slot(step) if step else slot(0, 1)
        return remote(src, dst, sems, kind, {"seq": peer})

    def send(*kinds):
        for kind in kinds:
            copy(kind, False).start()

    def wait(*kinds):
        for kind in kinds:
            copy(kind, True).wait_recv()

    def finish():
        for kind in range(11):
            copy(kind, False).wait_send()

    return slot, send, wait, finish


def head(
    hidden, gain, conv_w, conv_b, x_proj, dt_w, dt_b, a_log, skip, ssm_state, in_x, in_z, out_w,
    resid,
    wx, wz, wo, full, normed, xs, zs, u, share, heard, proj, step, dtx, bt, kept, y, states, gated, terms,
    tq, th, tvq, tvh,
    l_sem, h_sem, w_send, w_recv, g_send, g_recv, r_send, r_recv, c_send, c_recv, s_send, s_recv, t_send, t_recv,
):
    s, t, _, _ = here()
    loads = [
        pltpu.make_async_copy(src, dst.at[s], l_sem.at[i]) for i, (src, dst) in enumerate(((in_x, wx), (in_z, wz), (out_w, wo)))
    ]
    for load in loads:
        load.start()
    full[t, 16:272, :] = hidden[...]
    greet(range(1, 8), [(t + d) % 16 for d in range(1, 16)])

    slot, x_send, x_wait, x_done = gather_seq(in_x, wx, (w_send.at[0], w_recv.at[0]))
    _, z_send, z_wait, z_done = gather_seq(in_z, wz, (w_send.at[1], w_recv.at[1]))
    _, o_send, o_wait, o_done = gather_seq(out_w, wo, (w_send.at[2], w_recv.at[2]))

    halo = remote(hidden.at[240:256, :], full.at[t, 0:16, :], (h_sem.at[0], h_sem.at[1]), 0, {"seq": (s + 1) % 8})
    halo.start()
    x_send(0, 1, 2, 3)
    stages, gathered = gather_tp(full, ((144, 208, 272), (0, 80, 144)), (g_send, g_recv), halo.wait_recv)
    stages[0]()
    x_send(6)
    for stage in stages[1:4]:
        stage()
    x_wait(0)
    x_send(4)
    x_wait(1)
    x_send(5)
    for stage in stages[4:]:
        stage()

    def squares(k, total):
        wide = full[k].astype(jnp.float32)
        wide = wide * wide
        return total + (wide[:, 0:128] + wide[:, 128:256])

    total = lax.fori_loop(0, 16, squares, jnp.zeros((272, 128), jnp.float32))
    scale = lax.rsqrt(jnp.sum(total, axis=1, keepdims=True) * (1.0 / 4096.0) + EPS)

    def norm(k, _):
        cols = pl.ds(pl.multiple_of(k * 256, 256), 256)
        normed[:, cols] = (full[k].astype(jnp.float32) * scale * gain[:, cols]).astype(jnp.bfloat16)
        return 0

    lax.fori_loop(0, 16, norm, 0)

    def product(total, first, weight, k):
        cols = pl.ds(pl.multiple_of(k * 512, 512), 512)
        term = jnp.dot(normed[first:272, cols], weight[k], preferred_element_type=jnp.float32)
        total[...] = total[...] + term

    xs[...] = jnp.zeros_like(xs)
    loads[0].wait()
    product(xs, 0, wx, slot(0))
    x_wait(2, 3)
    x_send(7, 8)
    z_send(0, 1, 2, 3, 6)
    product(xs, 0, wx, slot(3))
    product(xs, 0, wx, slot(1))
    x_wait(4, 5)
    x_send(9, 10)
    o_send(0, 1, 2, 3, 6)
    product(xs, 0, wx, slot(2))
    x_wait(6, 7, 8)
    for dz in (0, 3, 1):
        product(xs, 0, wx, slot(dz, 1))
    x_wait(9, 10)
    product(xs, 0, wx, slot(2, 1))

    xs[...] = xs[...].astype(jnp.bfloat16).astype(jnp.float32)
    xs[0:16, :] = jnp.where(s > 0, xs[0:16, :], 0.0)
    total = conv_b[...]
    for tap in range(4):
        total = total + conv_w[tap : tap + 1, :] * xs[13 + tap : 269 + tap, :]
    u[...] = silu(total).astype(jnp.bfloat16)

    def projection(first, end):
        return lax.dot_general(
            u[...], x_proj[first:end, :], (((1,), (1,)), ((), ())), preferred_element_type=jnp.float32
        ).astype(jnp.bfloat16)

    low, rest = projection(0, 512), projection(512, 544)
    rest = jnp.concatenate([rest, jnp.zeros((256, 96), jnp.bfloat16)], axis=1)
    for g in range(16):
        share[g, :, 0:512] = low[16 * g : 16 * g + 16, :]
        share[g, :, 512:640] = rest[16 * g : 16 * g + 16, :]

    def give(d, arriving=False):
        peer = (t + d) % 16
        k = (t + 16 - d) % 16 if arriving else t
        return remote(share.at[peer], heard.at[k], (r_send, r_recv), d, {"tp": peer})

    def tell(d, arriving=False):
        peer = (t + d) % 16
        k = (t + 16 - d) % 16 if arriving else t
        return remote(proj.at[k], proj.at[k], (c_send, c_recv), d, {"tp": peer})

    def others(fn, count=16):
        lax.fori_loop(1, count, lambda d, _: (fn(d), 0)[1], 0)

    others(lambda d: give(d).start())
    heard[t] = share[t]
    others(lambda d: give(d, True).wait_recv())
    proj[t] = lax.fori_loop(
        0, 16, lambda k, total: total + heard[k].astype(jnp.float32), jnp.zeros((16, 640), jnp.float32)
    ).astype(jnp.bfloat16)
    others(lambda d: tell(d).start())
    z_wait(0)
    z_send(4)
    z_wait(1)
    z_send(5)
    others(lambda d: tell(d, True).wait_recv())

    low = proj[:, :, 0:512].reshape(256, 512)
    bc = proj[:, :, 512:640].reshape(256, 128).astype(jnp.float32)
    size = softplus(jnp.dot(low, dt_w[...], preferred_element_type=jnp.float32) + dt_b[...])
    step[...] = size
    dtx[...] = size * u[...].astype(jnp.float32)
    spread_b(bc, bt)
    rate = jnp.exp(a_log[...]) * (-LOG2E)
    states[s, 0:16, :] = jnp.exp2(rate * jnp.sum(size, axis=0, keepdims=True)).astype(jnp.bfloat16)
    states[s, 16:32, :] = run_states(step, dtx, bt, rate, jnp.zeros((16, 512), jnp.float32), None).astype(jnp.bfloat16)

    def pass_on(d, arriving=False):
        k = (s + 8 - d) % 8 if arriving else s
        return remote(states.at[k], states.at[k], (s_send, s_recv), d, {"seq": (s + d) % 8})

    lax.fori_loop(1, 8 - s, lambda d, _: (pass_on(d).start(), 0)[1], 0)
    z_wait(2, 3)
    z_send(7, 8)
    o_wait(0)
    o_send(4)
    o_wait(1)
    o_send(5)
    zs[...] = jnp.zeros_like(zs)
    loads[1].wait()
    for dz in (0, 3, 1):
        product(zs, 16, wz, slot(dz))
    z_wait(4, 5)
    z_send(9, 10)
    lax.fori_loop(1, s + 1, lambda d, _: (pass_on(d, True).wait_recv(), 0)[1], 0)

    def enter(k, state):
        return states[k, 0:16, :].astype(jnp.float32) * state + states[k, 16:32, :].astype(jnp.float32)

    start = lax.fori_loop(0, s, enter, ssm_state[...])
    run_states(step, dtx, bt, rate, start, kept)
    o_wait(2, 3)
    o_send(7, 8)
    c = block_c(bc)
    for g in range(16):
        y[16 * g : 16 * g + 16, :] = jnp.dot(
            c[16 * g : 16 * g + 16, :], kept[256 * g : 256 * g + 256, :], preferred_element_type=jnp.float32
        )
    z_wait(6, 7, 8, 9, 10)
    product(zs, 16, wz, slot(2))
    for dz in range(4):
        product(zs, 16, wz, slot(dz, 1))
    gate = silu(zs[...].astype(jnp.bfloat16).astype(jnp.float32))
    gated[...] = ((y[...] + skip[...] * u[...].astype(jnp.float32)) * gate).astype(jnp.bfloat16)
    loads[2].wait()
    o_wait(4, 5)
    o_send(9, 10)
    o_wait(6, 7, 8, 9, 10)

    def fill_terms(k):
        cols = pl.ds(pl.multiple_of(k % 2 * 256, 256), 256)
        terms[k] = jnp.dot(gated[...], wo[k // 2, :, cols], preferred_element_type=jnp.float32).astype(jnp.bfloat16)

    stages, terms_done = scatter_tp(terms, 0, 128, fill_terms, (tq, th, tvq, tvh), (t_send, t_recv))
    for stage in stages:
        stage()
    resid[...] = (hidden[...].astype(jnp.float32) + terms[t].astype(jnp.float32)).astype(jnp.bfloat16)

    halo.wait_send()
    gathered()
    x_done()
    z_done()
    o_done()
    others(lambda d: give(d).wait_send())
    others(lambda d: tell(d).wait_send())
    lax.fori_loop(1, 8 - s, lambda d, _: (pass_on(d).wait_send(), 0)[1], 0)
    terms_done()


def call_head(*args):
    vm, hbm = pl.BlockSpec(memory_space=pltpu.VMEM), pl.BlockSpec(memory_space=pl.ANY)
    b16, wide = jnp.bfloat16, jnp.float32
    dma = pltpu.SemaphoreType.DMA
    return pl.pallas_call(
        head,
        out_shape=bf16(256, 256),
        in_specs=[vm] * 10 + [hbm] * 3,
        out_specs=vm,
        scratch_shapes=[
            VMEM((8, 512, 512), b16), VMEM((8, 512, 512), b16), VMEM((8, 512, 512), b16),
            VMEM((16, 272, 256), b16), VMEM((272, 4096), b16), VMEM((272, 512), wide), VMEM((256, 512), wide),
            VMEM((256, 512), b16), VMEM((16, 16, 640), b16), VMEM((16, 16, 640), b16), VMEM((16, 16, 640), b16),
            VMEM((256, 512), wide), VMEM((256, 512), wide), VMEM((16, 16, 128), wide), VMEM((4096, 512), b16),
            VMEM((256, 512), wide), VMEM((8, 32, 512), b16), VMEM((256, 512), b16), VMEM((16, 256, 256), b16),
            *sum_bufs(128),
            dma((3,)), dma((2, 1)), dma((3, 11)), dma((3, 11)), dma((2, 20)), dma((2, 20)), dma((16,)), dma((16,)),
            dma((16,)), dma((16,)), dma((8,)), dma((8,)), dma((2, 20)), dma((2, 20)),
        ],
        compiler_params=pltpu.CompilerParams(collective_id=2, has_side_effects=True, vmem_limit_bytes=60 << 20),
    )(*args)


def local(
    hidden,
    expert_ids,
    expert_gates,
    mamba_gain,
    in_x_weight,
    in_z_weight,
    conv_weight,
    conv_bias,
    x_proj_weight,
    dt_weight,
    dt_bias,
    a_log,
    skip,
    ssm_state,
    out_weight,
    moe_gain,
    expert_gate,
    expert_up,
    expert_down,
):
    residual = call_head(
        hidden, mamba_gain[None], conv_weight, conv_bias[None], x_proj_weight.T, dt_weight, dt_bias[None], a_log, skip[None],
        ssm_state, in_x_weight, in_z_weight, out_weight,
    )
    return call_tail(residual, expert_ids.T, expert_gates.T, moe_gain[None], expert_gate, expert_up, expert_down)


def solution(mesh):
    placed = (
        P("seq", "tp"),
        P("seq", None),
        P("seq", None),
        P(),
        P("seq", "tp"),
        P("seq", "tp"),
        P(None, "tp"),
        P("tp"),
        P("tp", None),
        P(None, "tp"),
        P("tp"),
        P(None, "tp"),
        P("tp"),
        P(None, "tp"),
        P("tp", "seq"),
        P(),
        P("seq", None, "tp"),
        P("seq", None, "tp"),
        P("seq", "tp", None),
    )
    return jax.shard_map(local, mesh=mesh, in_specs=placed, out_specs=P("seq", "tp"), check_vma=False)
```

```python
import jax
import jax.numpy as jnp
from jax import lax
from jax.experimental import pallas as pl
from jax.experimental.pallas import tpu as pltpu
from jax.sharding import PartitionSpec as P

EPS = 1e-06
LOG2E = 1.4426950408889634
VMEM = pltpu.VMEM


def softplus(v):
    return jnp.maximum(v, 0.0) + jnp.log1p(jnp.exp(-jnp.abs(v)))


def silu(v):
    return v / (1.0 + jnp.exp(-v))


def spread_b(bc, bt_ref):
    flipped = bc.T
    for g in range(16):
        bt_ref[g, :, 0:16] = flipped[0:16, 16 * g : 16 * g + 16]


def block_c(bc):
    row = lax.broadcasted_iota(jnp.int32, (128, 256), 0)
    col = lax.broadcasted_iota(jnp.int32, (128, 256), 1)
    tile = jnp.where(row - 16 == col % 16, 1.0, 0.0).astype(jnp.bfloat16)
    wide = jnp.dot(bc.astype(jnp.bfloat16), tile, preferred_element_type=jnp.float32)
    row = lax.broadcasted_iota(jnp.int32, (256, 256), 0)
    col = lax.broadcasted_iota(jnp.int32, (256, 256), 1)
    return jnp.where(row % 16 == col // 16, wide, 0.0).astype(jnp.bfloat16)


def run_states(step_ref, dtx_ref, bt_ref, rate, start, keep):
    def group(g, state):
        rows = pl.ds(pl.multiple_of(g * 16, 16), 16)
        step = step_ref[rows, :]
        dtx = dtx_ref[rows, :]
        b = bt_ref[g]
        for j in range(16):
            decay = jnp.exp2(step[j : j + 1, :] * rate)
            state = decay * state + b[:, j : j + 1] * dtx[j : j + 1, :]
            if keep is not None:
                keep[pl.ds(pl.multiple_of(g * 256 + 16 * j, 16), 16), :] = state.astype(jnp.bfloat16)
        return state

    return lax.fori_loop(0, 16, group, start)


def bf16(*shape):
    return jax.ShapeDtypeStruct(shape, jnp.bfloat16)


MESH = pl.DeviceIdType.MESH


def here():
    s, t = lax.axis_index("seq"), lax.axis_index("tp")
    return s, t, t // 4, t % 4


def remote(src, dst, sems, kind, device):
    return pltpu.make_async_remote_copy(
        src_ref=src,
        dst_ref=dst,
        send_sem=sems[0].at[kind],
        recv_sem=sems[1].at[kind],
        device_id=device,
        device_id_type=MESH,
    )


def slot_of(h, f, g):
    _, _, y, x = here()
    dy, dx = (g, f) if h == 0 else (f, g)
    return (y + dy) % 4 * 4 + (x + dx) % 4


def f_peer(h, d):
    return {"tp": slot_of(h, d, 0)}


def g_peer(h, d):
    return {"tp": slot_of(h, 0, d)}


def greet(seq_steps, tp_peers=None):
    s, _, _, _ = here()
    barrier = pltpu.get_barrier_semaphore()
    peers = [f_peer(0, 1), f_peer(0, 3), g_peer(0, 1), g_peer(0, 3)]
    if tp_peers is not None:
        peers = [{"tp": peer} for peer in tp_peers]
    peers += [{"seq": (s + d) % 8} for d in seq_steps]
    for peer in peers:
        pl.semaphore_signal(barrier, inc=1, device_id=peer, device_id_type=MESH)
    pl.semaphore_wait(barrier, len(peers))


def gather_tp(full, halves, sems, ready=lambda: None):
    def part(h, f, g, piece):
        lo, mid, hi = halves[h]
        a, b = {"h": (lo, hi), "q1": (lo, mid), "q2": (mid, hi)}[piece]
        return full.at[slot_of(h, f, g), a:b, :]

    def move(h, axis, f, piece, out, kind):
        d = 1 if kind in (0, 2) else 3
        if axis == "f":
            ref = part(h, out, 0, piece)
            return remote(ref, ref, (sems[0].at[h], sems[1].at[h]), 16 + kind, f_peer(h, d))
        ref = part(h, f, out, piece)
        return remote(ref, ref, (sems[0].at[h], sems[1].at[h]), f * 4 + kind, g_peer(h, d))

    def send(h, axis, f, kind):
        off = {0: 0, 1: 0, 2: 3, 3: 1}[kind]
        move(h, axis, f, {0: "h", 1: "h", 2: "q1", 3: "q2"}[kind], off, kind).start()

    def arrived(h, axis, f, kind):
        off = {0: 3, 1: 1, 2: 2, 3: 2}[kind]
        move(h, axis, f, {0: "h", 1: "h", 2: "q1", 3: "q2"}[kind], off, kind).wait_recv()

    def sent(h, axis, f, kind):
        off = {0: 0, 1: 0, 2: 3, 3: 1}[kind]
        move(h, axis, f, {0: "h", 1: "h", 2: "q1", 3: "q2"}[kind], off, kind).wait_send()

    def begin(h):
        for kind in (0, 1):
            send(h, "f", 0, kind)
        for kind in (0, 1):
            send(h, "g", 0, kind)

    def second(h):
        for kind, f in ((0, 3), (1, 1)):
            arrived(h, "f", 0, kind)
            send(h, "f", 0, kind + 2)
            send(h, "g", f, 0)
            send(h, "g", f, 1)

    def onward(h, f):
        for kind in (0, 1):
            arrived(h, "g", f, kind)
            send(h, "g", f, kind + 2)

    def third(h):
        for kind in (2, 3):
            arrived(h, "f", 0, kind)
        send(h, "g", 2, 0)
        send(h, "g", 2, 1)

    def last(h):
        for f in range(4):
            for kind in (2, 3):
                arrived(h, "g", f, kind)

    def finish():
        for h in (0, 1):
            for kind in range(4):
                sent(h, "f", 0, kind)
            for f in range(4):
                for kind in range(4):
                    sent(h, "g", f, kind)

    stages = [
        lambda: [begin(0), ready(), begin(1)],
        lambda: [second(h) for h in (0, 1)],
        lambda: [onward(h, 0) for h in (0, 1)],
        lambda: [third(h) for h in (0, 1)],
        lambda: [onward(h, f) for f in (3, 1) for h in (0, 1)],
        lambda: [onward(h, 2) for h in (0, 1)],
        lambda: [last(h) for h in (0, 1)],
    ]
    return stages, finish


def add_to(ref, *others):
    total = ref[...].astype(jnp.float32)
    for other in others:
        total = total + other[...].astype(jnp.float32)
    ref[...] = total.astype(jnp.bfloat16)


def scatter_tp(part, first, half, fill, bufs, sems):
    uq, uh, vq, vh = bufs
    quarter = half // 2

    def rows(h, piece):
        lo = first + h * half
        a, b = {"h": (lo, lo + half), "q1": (lo, lo + quarter), "q2": (lo + quarter, lo + half)}[piece]
        return slice(a, b)

    def spot(h, f, g, piece):
        return part.at[slot_of(h, f, g), rows(h, piece), :]

    names = ("q1", "q2", "h", "h")
    offs = (2, 2, 1, 3)

    def u_move(h, f, kind):
        dst = uq.at[h, f, kind] if kind < 2 else uh.at[h, f, kind - 2]
        src = spot(h, f, offs[kind], names[kind])
        return remote(src, dst, (sems[0].at[h], sems[1].at[h]), f * 4 + kind, g_peer(h, 1 if kind % 2 == 0 else 3))

    def v_move(h, kind):
        dst = vq.at[h, kind] if kind < 2 else vh.at[h, kind - 2]
        src = spot(h, offs[kind], 0, names[kind])
        return remote(src, dst, (sems[0].at[h], sems[1].at[h]), 16 + kind, f_peer(h, 1 if kind % 2 == 0 else 3))

    def each(fn):
        for h in (0, 1):
            lax.fori_loop(0, 4, lambda f, _, h=h: (fn(h, f), 0)[1], 0)

    def step1():
        def far_rows(f, _):
            fill(slot_of(0, f, 2))
            u_move(0, f, 0).start()
            u_move(0, f, 1).start()
            return 0

        lax.fori_loop(0, 4, far_rows, 0)
        for f in (2, 0, 1, 3):
            if f != 2:
                fill(slot_of(1, f, 2))
            u_move(1, f, 0).start()
            u_move(1, f, 1).start()

    def made():
        def near(i, _):
            f, g = i // 3 + i // 6, i % 3 + i % 3 // 2
            fill(slot_of(0, f, g))
            return 0

        lax.fori_loop(0, 9, near, 0)

    def pass_on(h, f):
        for kind, g, piece in ((0, 1, "q1"), (1, 3, "q2")):
            u_move(h, f, kind).wait_recv()
            add_to(spot(h, f, g, piece), uq.at[h, f, kind])
            u_move(h, f, kind + 2).start()

    def summed(h, f):
        u_move(h, f, 2).wait_recv()
        u_move(h, f, 3).wait_recv()
        add_to(spot(h, f, 0, "h"), uh.at[h, f, 0], uh.at[h, f, 1])

    def far():
        for h in (0, 1):
            summed(h, 2)
            v_move(h, 0).start()
            v_move(h, 1).start()

    def sides():
        for f, kind, piece in ((1, 0, "q1"), (3, 1, "q2")):
            for h in (0, 1):
                summed(h, f)
                v_move(h, kind).wait_recv()
                add_to(spot(h, f, 0, piece), vq.at[h, kind])
                v_move(h, kind + 2).start()

    def own():
        for h in (0, 1):
            summed(h, 0)

    def last():
        for h in (0, 1):
            v_move(h, 2).wait_recv()
            v_move(h, 3).wait_recv()
            add_to(spot(h, 0, 0, "h"), vh.at[h, 0], vh.at[h, 1])

    def finish():
        def u_sent(h, f):
            for kind in range(4):
                u_move(h, f, kind).wait_send()

        each(u_sent)
        for h in (0, 1):
            for kind in range(4):
                v_move(h, kind).wait_send()

    return [step1, made, lambda: each(pass_on), far, sides, own, last], finish


def sum_bufs(half):
    b16, q = jnp.bfloat16, half // 2
    return [
        VMEM((2, 4, 2, q, 256), b16), VMEM((2, 4, 2, half, 256), b16), VMEM((2, 2, q, 256), b16), VMEM((2, 2, half, 256), b16)
    ]


def gather_seq(own, block, sems):
    s, _, _, _ = here()
    z, core = s // 2, s % 2

    def slot(dz, other=0):
        return (z + dz) % 4 * 2 + (core + other) % 2

    rows = {"q1": slice(0, 256), "q2": slice(256, 512), "all": slice(0, 512)}
    plan = [
        (0, "q1", 1), (0, "q2", 3), (0, "q2", 1), (0, "q1", 3), (3, "q1", 1), (1, "q2", 3),
        (0, "all", 0), (3, "all", 0), (1, "all", 0), (2, "q1", 0), (2, "q2", 0),
    ]

    def copy(kind, arriving):
        dz, piece, step = plan[kind]
        k = slot((dz - step) % 4, 0 if step else 1) if arriving else slot(dz)
        dst = block(k, rows[piece])
        src = own.at[rows[piece], :] if dz == 0 and not arriving else dst
        peer = slot(step) if step else slot(0, 1)
        return remote(src, dst, sems, kind, {"seq": peer})

    def send(*kinds):
        for kind in kinds:
            copy(kind, False).start()

    def wait(*kinds):
        for kind in kinds:
            copy(kind, True).wait_recv()

    def finish():
        for kind in range(11):
            copy(kind, False).wait_send()

    return slot, send, wait, finish


ORDER = (0, 1, 7, 2, 6, 3, 5, 4)


def layer(
    hidden, gain, conv_w, conv_b, x_proj, dt_w, dt_b, a_log, skip, ssm_state, ids, gates, moe_gain,
    in_x, in_z, out_w, gate_hbm, up_hbm, down_hbm,
    out,
    resid, first, scaled, xs, zs, u, share, heard, proj, step, dtx, bt, y, states, gated, terms, tq, th, tvq, tvh,
    gate_w, up_w, down_w, outgoing, full, normed, active, parts, back, places, pq, ph, pvq, pvh, rq, rh, rvq, rvh,
    l_sem, h_sem, w_send, w_recv, f_send, f_recv, r_send, r_recv, c_send, c_recv, s_send, s_recv, t_send, t_recv,
    e_sem, g_send, g_recv, p_send, p_recv, a_send, a_recv, b_send, b_recv,
):
    s, t, _, _ = here()
    def beside(ref):
        return lambda k, rows: ref.at[rows, pl.ds(pl.multiple_of(k * 512, 512), 512)]

    def stacked(ref):
        return lambda k, rows: ref.at[pl.ds(pl.multiple_of(k * 512 + rows.start, 256), rows.stop - rows.start), 0:512]

    x_block, z_block, o_block = beside(normed), beside(down_w), stacked(gate_w)
    kept = up_w.at[:, 0:512]
    fetch = [
        pltpu.make_async_copy(src.at[0], dst, e_sem.at[i])
        for i, (src, dst) in enumerate(((gate_hbm, gate_w), (up_hbm, up_w), (down_hbm, down_w)))
    ]
    loads = [
        pltpu.make_async_copy(src, block(s, slice(0, 512)), l_sem.at[i])
        for i, (src, block) in enumerate(((in_x, x_block), (in_z, z_block), (out_w, o_block)))
    ]
    for load in loads:
        load.start()
    first[t, 16:272, :] = hidden[...]
    name = lax.broadcasted_iota(jnp.int32, (16, 256), 0)
    either = jnp.where((name == ids[0:1, :]) | (name == ids[1:2, :]), 1.0, 0.0).astype(jnp.bfloat16)
    row = lax.broadcasted_iota(jnp.int32, (256, 256), 0)
    col = lax.broadcasted_iota(jnp.int32, (256, 256), 1)
    before = jnp.where(row < col, 1.0, 0.0).astype(jnp.bfloat16)
    slots = jnp.dot(either, before, preferred_element_type=jnp.float32)
    line = lax.broadcasted_iota(jnp.int32, (768, 256), 0).astype(jnp.float32)

    def place(k):
        mine = ids[k : k + 1, :]
        target = jnp.sum(jnp.where(name == mine, slots, 0.0), axis=0, keepdims=True) + 96.0 * mine.astype(jnp.float32)
        return jnp.where(line == target, 1.0, 0.0)

    places[0] = place(0).astype(jnp.bfloat16)
    places[1] = place(1).astype(jnp.bfloat16)
    greet(range(1, 8), [(t + d) % 16 for d in range(1, 16)])

    slot, x_send, x_wait, x_done = gather_seq(in_x, x_block, (w_send.at[0], w_recv.at[0]))
    _, z_send, z_wait, z_done = gather_seq(in_z, z_block, (w_send.at[1], w_recv.at[1]))
    _, o_send, o_wait, o_done = gather_seq(out_w, o_block, (w_send.at[2], w_recv.at[2]))

    halo = remote(hidden.at[240:256, :], first.at[t, 0:16, :], (h_sem.at[0], h_sem.at[1]), 0, {"seq": (s + 1) % 8})
    halo.start()
    x_send(0, 1, 2, 3)
    stages, gathered = gather_tp(first, ((144, 208, 272), (0, 80, 144)), (f_send, f_recv), halo.wait_recv)
    stages[0]()
    x_send(6)
    for stage in stages[1:4]:
        stage()
    x_wait(0)
    x_send(4)
    x_wait(1)
    x_send(5)
    for stage in stages[4:]:
        stage()

    x_wait(2, 3)
    x_send(7, 8)
    z_send(0, 1, 2, 3, 6)

    def squares(k, total):
        wide = first[k].astype(jnp.float32)
        wide = wide * wide
        return total + (wide[:, 0:128] + wide[:, 128:256])

    total = lax.fori_loop(0, 16, squares, jnp.zeros((272, 128), jnp.float32))
    scale = lax.rsqrt(jnp.sum(total, axis=1, keepdims=True) * (1.0 / 4096.0) + EPS)

    def norm(k, _):
        cols = pl.ds(pl.multiple_of(k * 256, 256), 256)
        scaled[:, cols] = (first[k].astype(jnp.float32) * scale * gain[:, cols]).astype(jnp.bfloat16)
        return 0

    lax.fori_loop(0, 16, norm, 0)

    def product(total, top, weight, k):
        cols = pl.ds(pl.multiple_of(k * 512, 512), 512)
        term = jnp.dot(scaled[top:272, cols], weight(k, slice(0, 512))[...], preferred_element_type=jnp.float32)
        total[...] = total[...] + term

    xs[...] = jnp.zeros_like(xs)
    loads[0].wait()
    product(xs, 0, x_block, slot(0))
    product(xs, 0, x_block, slot(3))
    product(xs, 0, x_block, slot(1))
    x_wait(4, 5)
    x_send(9, 10)
    o_send(0, 1, 2, 3, 6)
    product(xs, 0, x_block, slot(2))
    x_wait(6, 7, 8)
    for dz in (0, 3, 1):
        product(xs, 0, x_block, slot(dz, 1))
    x_wait(9, 10)
    product(xs, 0, x_block, slot(2, 1))

    xs[...] = xs[...].astype(jnp.bfloat16).astype(jnp.float32)
    xs[0:16, :] = jnp.where(s > 0, xs[0:16, :], 0.0)
    total = conv_b[...]
    for tap in range(4):
        total = total + conv_w[tap : tap + 1, :] * xs[13 + tap : 269 + tap, :]
    u[...] = silu(total).astype(jnp.bfloat16)

    def projection(first, end):
        return lax.dot_general(
            u[...], x_proj[first:end, :], (((1,), (1,)), ((), ())), preferred_element_type=jnp.float32
        ).astype(jnp.bfloat16)

    low, rest = projection(0, 512), projection(512, 544)
    rest = jnp.concatenate([rest, jnp.zeros((256, 96), jnp.bfloat16)], axis=1)
    for g in range(16):
        share[g, :, 0:512] = low[16 * g : 16 * g + 16, :]
        share[g, :, 512:640] = rest[16 * g : 16 * g + 16, :]

    def give(d, arriving=False):
        peer = (t + d) % 16
        k = (t + 16 - d) % 16 if arriving else t
        return remote(share.at[peer], heard.at[k], (r_send, r_recv), d, {"tp": peer})

    def tell(d, arriving=False):
        peer = (t + d) % 16
        k = (t + 16 - d) % 16 if arriving else t
        return remote(proj.at[k], proj.at[k], (c_send, c_recv), d, {"tp": peer})

    def others(fn, count=16):
        lax.fori_loop(1, count, lambda d, _: (fn(d), 0)[1], 0)

    others(lambda d: give(d).start())
    heard[t] = share[t]
    others(lambda d: give(d, True).wait_recv())
    proj[t] = lax.fori_loop(
        0, 16, lambda k, total: total + heard[k].astype(jnp.float32), jnp.zeros((16, 640), jnp.float32)
    ).astype(jnp.bfloat16)
    others(lambda d: tell(d).start())
    z_wait(0)
    z_send(4)
    z_wait(1)
    z_send(5)
    others(lambda d: tell(d, True).wait_recv())

    low = proj[:, :, 0:512].reshape(256, 512)
    bc = proj[:, :, 512:640].reshape(256, 128).astype(jnp.float32)
    size = softplus(jnp.dot(low, dt_w[...], preferred_element_type=jnp.float32) + dt_b[...])
    step[...] = size
    dtx[...] = size * u[...].astype(jnp.float32)
    spread_b(bc, bt)
    rate = jnp.exp(a_log[...]) * (-LOG2E)
    states[s, 0:16, :] = jnp.exp2(rate * jnp.sum(size, axis=0, keepdims=True)).astype(jnp.bfloat16)
    states[s, 16:32, :] = run_states(step, dtx, bt, rate, jnp.zeros((16, 512), jnp.float32), None).astype(jnp.bfloat16)

    def pass_on(d, arriving=False):
        k = (s + 8 - d) % 8 if arriving else s
        return remote(states.at[k], states.at[k], (s_send, s_recv), d, {"seq": (s + d) % 8})

    lax.fori_loop(1, 8 - s, lambda d, _: (pass_on(d).start(), 0)[1], 0)
    z_wait(2, 3)
    z_send(7, 8)
    o_wait(0)
    o_send(4)
    o_wait(1)
    o_send(5)
    zs[...] = jnp.zeros_like(zs)
    loads[1].wait()
    for dz in (0, 3, 1):
        product(zs, 16, z_block, slot(dz))
    z_wait(4, 5)
    z_send(9, 10)
    lax.fori_loop(1, s + 1, lambda d, _: (pass_on(d, True).wait_recv(), 0)[1], 0)

    def enter(k, state):
        return states[k, 0:16, :].astype(jnp.float32) * state + states[k, 16:32, :].astype(jnp.float32)

    start = lax.fori_loop(0, s, enter, ssm_state[...])
    run_states(step, dtx, bt, rate, start, kept)
    o_wait(2, 3)
    o_send(7, 8)
    c = block_c(bc)
    for g in range(16):
        y[16 * g : 16 * g + 16, :] = jnp.dot(
            c[16 * g : 16 * g + 16, :], kept[256 * g : 256 * g + 256, :], preferred_element_type=jnp.float32
        )
    fetch[1].start()
    z_wait(6, 7, 8, 9, 10)
    product(zs, 16, z_block, slot(2))
    for dz in range(4):
        product(zs, 16, z_block, slot(dz, 1))
    z_done()
    fetch[2].start()
    gate = silu(zs[...].astype(jnp.bfloat16).astype(jnp.float32))
    gated[...] = ((y[...] + skip[...] * u[...].astype(jnp.float32)) * gate).astype(jnp.bfloat16)
    loads[2].wait()
    o_wait(4, 5)
    o_send(9, 10)
    o_wait(6, 7, 8, 9, 10)

    def fill_terms(k):
        rows = pl.ds(pl.multiple_of(k // 2 * 512, 512), 512)
        cols = pl.ds(pl.multiple_of(k % 2 * 256, 256), 256)
        terms[k] = jnp.dot(gated[...], gate_w[rows, cols], preferred_element_type=jnp.float32).astype(jnp.bfloat16)

    stages, terms_done = scatter_tp(terms, 0, 128, fill_terms, (tq, th, tvq, tvh), (t_send, t_recv))
    stages[0]()
    stages[1]()
    o_done()
    fetch[0].start()
    for stage in stages[2:]:
        stage()
    resid[...] = (hidden[...].astype(jnp.float32) + terms[t].astype(jnp.float32)).astype(jnp.bfloat16)


    outgoing[...] = jnp.dot(places[0] + places[1], resid[...], preferred_element_type=jnp.float32).astype(jnp.bfloat16)

    def mine(ref, k):
        return ref.at[pl.ds(pl.multiple_of(k * 96, 16), 96), :]

    def there(i):
        d = ORDER[i]
        peer = (s + d) % 8
        return remote(mine(outgoing, peer), mine(full.at[t], i), (a_send, a_recv), i, {"seq": peer})

    for i in range(1, 8):
        there(i).start()
    full[t, 0:96, :] = mine(outgoing, s)[...]

    spread, spread_done = zip(
        *[
            gather_tp(
                full,
                ((c * 384, c * 384 + 96, c * 384 + 192), (c * 384 + 192, c * 384 + 288, c * 384 + 384)),
                (g_send.at[c], g_recv.at[c]),
            )
            for c in (0, 1)
        ]
    )

    def chunk_norm(c):
        rows = slice(c * 384, c * 384 + 384)

        def squares(k, total):
            wide = full[k, rows, :].astype(jnp.float32)
            wide = wide * wide
            return total + (wide[:, 0:128] + wide[:, 128:256])

        total = lax.fori_loop(0, 16, squares, jnp.zeros((384, 128), jnp.float32))
        scale = lax.rsqrt(jnp.sum(total, axis=1, keepdims=True) * (1.0 / 4096.0) + EPS)

        def apply(k, _):
            cols = pl.ds(pl.multiple_of(k * 256, 256), 256)
            normed[rows, cols] = (full[k, rows, :].astype(jnp.float32) * scale * moe_gain[:, cols]).astype(jnp.bfloat16)
            return 0

        lax.fori_loop(0, 16, apply, 0)

    def hidden_units(c, j):
        rows, cols = slice(c * 384, c * 384 + 384), slice(j * 256, j * 256 + 256)
        a = jnp.dot(normed[rows, :], gate_w[:, cols], preferred_element_type=jnp.float32)
        b = jnp.dot(normed[rows, :], up_w[:, cols], preferred_element_type=jnp.float32)
        active[rows, cols] = (silu(a) * b).astype(jnp.bfloat16)

    def fill_parts(c):
        rows = slice(c * 384, c * 384 + 384)

        def fill(slot):
            cols = pl.ds(pl.multiple_of(slot * 256, 256), 256)
            parts[slot, rows, :] = jnp.dot(
                active[rows, :], down_w[:, cols], preferred_element_type=jnp.float32
            ).astype(jnp.bfloat16)

        return fill

    sums = ((pq, ph, pvq, pvh), (rq, rh, rvq, rvh))
    part, part_done = zip(
        *[scatter_tp(parts, c * 384, 192, fill_parts(c), sums[c], (p_send.at[c], p_recv.at[c])) for c in (0, 1)]
    )

    def home(i):
        peer = (s + 8 - ORDER[i]) % 8
        return remote(mine(parts.at[t], i), mine(back, s), (b_send, b_recv), i, {"seq": peer})

    def run(stages, *which):
        for i in which:
            stages[i]()

    for i in (1, 2, 3):
        there(i).wait_recv()
    run(spread[0], 0, 1)
    for i in (4, 5, 6, 7):
        there(i).wait_recv()
    run(spread[1], 0)
    run(spread[0], 2, 3)
    run(spread[1], 1)
    run(spread[0], 4)
    run(spread[1], 2)
    run(spread[0], 5)
    run(spread[1], 3)
    run(spread[0], 6)
    x_done()
    chunk_norm(0)
    run(spread[1], 4)
    fetch[0].wait()
    fetch[1].wait()
    hidden_units(0, 0)
    run(spread[1], 5)
    hidden_units(0, 1)
    hidden_units(0, 2)
    fetch[2].wait()
    run(part[0], 0)
    run(spread[1], 6)
    run(part[0], 1, 2)
    chunk_norm(1)
    hidden_units(1, 0)
    run(part[0], 3)
    hidden_units(1, 1)
    run(part[0], 4)
    hidden_units(1, 2)
    run(part[1], 0)
    run(part[0], 5, 6)
    for i in (1, 2, 3):
        home(i).start()
    mine(back, s)[...] = parts[t, 0:96, :]
    run(part[1], 1, 2, 3, 4, 5, 6)
    for i in (4, 5, 6, 7):
        home(i).start()
    fine = [gates[k : k + 1, :] for k in (0, 1)]
    high = [g.astype(jnp.bfloat16).astype(jnp.float32) for g in fine]
    result = resid[...].astype(jnp.float32)
    wide = [places[k].astype(jnp.float32) for k in (0, 1)]
    weigh = [
        (wide[0] * g[0] + wide[1] * g[1]).astype(jnp.bfloat16) for g in (high, [fine[k] - high[k] for k in (0, 1)])
    ]
    for i in range(1, 8):
        home(i).wait_recv()
    for w in weigh:
        result = result + lax.dot_general(
            w, back[...], (((0,), (0,)), ((), ())), preferred_element_type=jnp.float32
        )
    out[...] = result.astype(jnp.bfloat16)

    for c in (0, 1):
        spread_done[c]()
        part_done[c]()
    for i in range(1, 8):
        there(i).wait_send()
        home(i).wait_send()
    halo.wait_send()
    gathered()
    others(lambda d: give(d).wait_send())
    others(lambda d: tell(d).wait_send())
    lax.fori_loop(1, 8 - s, lambda d, _: (pass_on(d).wait_send(), 0)[1], 0)
    terms_done()


def call_layer(*args):
    vm, hbm = pl.BlockSpec(memory_space=pltpu.VMEM), pl.BlockSpec(memory_space=pl.ANY)
    b16, wide = jnp.bfloat16, jnp.float32
    dma = pltpu.SemaphoreType.DMA
    return pl.pallas_call(
        layer,
        out_shape=bf16(256, 256),
        in_specs=[vm] * 13 + [hbm] * 6,
        out_specs=vm,
        scratch_shapes=[
            VMEM((256, 256), b16), VMEM((16, 272, 256), b16), VMEM((272, 4096), b16), VMEM((272, 512), wide),
            VMEM((256, 512), wide), VMEM((256, 512), b16), VMEM((16, 16, 640), b16), VMEM((16, 16, 640), b16),
            VMEM((16, 16, 640), b16), VMEM((256, 512), wide), VMEM((256, 512), wide), VMEM((16, 16, 128), wide),
            VMEM((256, 512), wide), VMEM((8, 32, 512), b16), VMEM((256, 512), b16), VMEM((16, 256, 256), b16),
            *sum_bufs(128),
            VMEM((4096, 768), b16), VMEM((4096, 768), b16), VMEM((768, 4096), b16),
            VMEM((768, 256), b16), VMEM((16, 768, 256), b16), VMEM((768, 4096), b16),
            VMEM((768, 768), b16), VMEM((16, 768, 256), b16), VMEM((768, 256), b16), VMEM((2, 768, 256), b16),
            *sum_bufs(192), *sum_bufs(192),
            dma((3,)), dma((2, 1)), dma((3, 11)), dma((3, 11)), dma((2, 20)), dma((2, 20)), dma((16,)), dma((16,)),
            dma((16,)), dma((16,)), dma((8,)), dma((8,)), dma((2, 20)), dma((2, 20)),
            dma((3,)), dma((2, 2, 20)), dma((2, 2, 20)), dma((2, 2, 20)), dma((2, 2, 20)),
            dma((8,)), dma((8,)), dma((8,)), dma((8,)),
        ],
        compiler_params=pltpu.CompilerParams(collective_id=1, has_side_effects=True, vmem_limit_bytes=62 << 20),
    )(*args)


def local(
    hidden,
    expert_ids,
    expert_gates,
    mamba_gain,
    in_x_weight,
    in_z_weight,
    conv_weight,
    conv_bias,
    x_proj_weight,
    dt_weight,
    dt_bias,
    a_log,
    skip,
    ssm_state,
    out_weight,
    moe_gain,
    expert_gate,
    expert_up,
    expert_down,
):
    return call_layer(
        hidden, mamba_gain[None], conv_weight, conv_bias[None], x_proj_weight.T, dt_weight, dt_bias[None], a_log, skip[None],
        ssm_state, expert_ids.T, expert_gates.T, moe_gain[None], in_x_weight, in_z_weight, out_weight, expert_gate,
        expert_up, expert_down,
    )


def solution(mesh):
    placed = (
        P("seq", "tp"),
        P("seq", None),
        P("seq", None),
        P(),
        P("seq", "tp"),
        P("seq", "tp"),
        P(None, "tp"),
        P("tp"),
        P("tp", None),
        P(None, "tp"),
        P("tp"),
        P(None, "tp"),
        P("tp"),
        P(None, "tp"),
        P("tp", "seq"),
        P(),
        P("seq", None, "tp"),
        P("seq", None, "tp"),
        P("seq", "tp", None),
    )
    return jax.shard_map(local, mesh=mesh, in_specs=placed, out_specs=P("seq", "tp"), check_vma=False)
```

```python
import jax
import jax.numpy as jnp
from jax import lax
from jax.experimental import pallas as pl
from jax.experimental.pallas import tpu as pltpu
from jax.sharding import PartitionSpec as P

EPS = 1e-06
LOG2E = 1.4426950408889634
VMEM = pltpu.VMEM


def softplus(v):
    return jnp.maximum(v, 0.0) + jnp.log1p(jnp.exp(-jnp.abs(v)))


def silu(v):
    return v / (1.0 + jnp.exp(-v))


def spread_b(bc, bt_ref):
    flipped = bc.T
    for g in range(16):
        bt_ref[g, :, 0:16] = flipped[0:16, 16 * g : 16 * g + 16]


def block_c(bc):
    row = lax.broadcasted_iota(jnp.int32, (128, 256), 0)
    col = lax.broadcasted_iota(jnp.int32, (128, 256), 1)
    tile = jnp.where(row - 16 == col % 16, 1.0, 0.0).astype(jnp.bfloat16)
    wide = jnp.dot(bc.astype(jnp.bfloat16), tile, preferred_element_type=jnp.float32)
    row = lax.broadcasted_iota(jnp.int32, (256, 256), 0)
    col = lax.broadcasted_iota(jnp.int32, (256, 256), 1)
    return jnp.where(row % 16 == col // 16, wide, 0.0).astype(jnp.bfloat16)


def run_states(step_ref, dtx_ref, bt_ref, rate, start, keep):
    def group(g, state):
        rows = pl.ds(pl.multiple_of(g * 16, 16), 16)
        step = step_ref[rows, :]
        dtx = dtx_ref[rows, :]
        b = bt_ref[g]
        for j in range(16):
            decay = jnp.exp2(step[j : j + 1, :] * rate)
            state = decay * state + b[:, j : j + 1] * dtx[j : j + 1, :]
            if keep is not None:
                keep[pl.ds(pl.multiple_of(g * 256 + 16 * j, 16), 16), :] = state.astype(jnp.bfloat16)
        return state

    return lax.fori_loop(0, 16, group, start)


def bf16(*shape):
    return jax.ShapeDtypeStruct(shape, jnp.bfloat16)


MESH = pl.DeviceIdType.MESH


def here():
    s, t = lax.axis_index("seq"), lax.axis_index("tp")
    return s, t, t // 4, t % 4


def remote(src, dst, sems, kind, device):
    return pltpu.make_async_remote_copy(
        src_ref=src,
        dst_ref=dst,
        send_sem=sems[0].at[kind],
        recv_sem=sems[1].at[kind],
        device_id=device,
        device_id_type=MESH,
    )


def slot_of(h, f, g):
    _, _, y, x = here()
    dy, dx = (g, f) if h == 0 else (f, g)
    return (y + dy) % 4 * 4 + (x + dx) % 4


def f_peer(h, d):
    return {"tp": slot_of(h, d, 0)}


def g_peer(h, d):
    return {"tp": slot_of(h, 0, d)}


def greet(seq_steps, tp_peers=None):
    s, _, _, _ = here()
    barrier = pltpu.get_barrier_semaphore()
    peers = [f_peer(0, 1), f_peer(0, 3), g_peer(0, 1), g_peer(0, 3)]
    if tp_peers is not None:
        peers = [{"tp": peer} for peer in tp_peers]
    peers += [{"seq": (s + d) % 8} for d in seq_steps]
    for peer in peers:
        pl.semaphore_signal(barrier, inc=1, device_id=peer, device_id_type=MESH)
    pl.semaphore_wait(barrier, len(peers))


def gather_tp(full, halves, sems, ready=lambda: None):
    def part(h, f, g, piece):
        lo, mid, hi = halves[h]
        a, b = {"h": (lo, hi), "q1": (lo, mid), "q2": (mid, hi)}[piece]
        return full.at[slot_of(h, f, g), a:b, :]

    def move(h, axis, f, piece, out, kind):
        d = 1 if kind in (0, 2) else 3
        if axis == "f":
            ref = part(h, out, 0, piece)
            return remote(ref, ref, (sems[0].at[h], sems[1].at[h]), 16 + kind, f_peer(h, d))
        ref = part(h, f, out, piece)
        return remote(ref, ref, (sems[0].at[h], sems[1].at[h]), f * 4 + kind, g_peer(h, d))

    def send(h, axis, f, kind):
        off = {0: 0, 1: 0, 2: 3, 3: 1}[kind]
        move(h, axis, f, {0: "h", 1: "h", 2: "q1", 3: "q2"}[kind], off, kind).start()

    def arrived(h, axis, f, kind):
        off = {0: 3, 1: 1, 2: 2, 3: 2}[kind]
        move(h, axis, f, {0: "h", 1: "h", 2: "q1", 3: "q2"}[kind], off, kind).wait_recv()

    def sent(h, axis, f, kind):
        off = {0: 0, 1: 0, 2: 3, 3: 1}[kind]
        move(h, axis, f, {0: "h", 1: "h", 2: "q1", 3: "q2"}[kind], off, kind).wait_send()

    def begin(h):
        for kind in (0, 1):
            send(h, "f", 0, kind)
        for kind in (0, 1):
            send(h, "g", 0, kind)

    def second(h):
        for kind, f in ((0, 3), (1, 1)):
            arrived(h, "f", 0, kind)
            send(h, "f", 0, kind + 2)
            send(h, "g", f, 0)
            send(h, "g", f, 1)

    def onward(h, f):
        for kind in (0, 1):
            arrived(h, "g", f, kind)
            send(h, "g", f, kind + 2)

    def third(h):
        for kind in (2, 3):
            arrived(h, "f", 0, kind)
        send(h, "g", 2, 0)
        send(h, "g", 2, 1)

    def last(h):
        for f in range(4):
            for kind in (2, 3):
                arrived(h, "g", f, kind)

    def finish():
        for h in (0, 1):
            for kind in range(4):
                sent(h, "f", 0, kind)
            for f in range(4):
                for kind in range(4):
                    sent(h, "g", f, kind)

    stages = [
        lambda: [begin(0), ready(), begin(1)],
        lambda: [second(h) for h in (0, 1)],
        lambda: [onward(h, 0) for h in (0, 1)],
        lambda: [third(h) for h in (0, 1)],
        lambda: [onward(h, f) for f in (3, 1) for h in (0, 1)],
        lambda: [onward(h, 2) for h in (0, 1)],
        lambda: [last(h) for h in (0, 1)],
    ]
    return stages, finish


def add_to(ref, *others):
    total = ref[...].astype(jnp.float32)
    for other in others:
        total = total + other[...].astype(jnp.float32)
    ref[...] = total.astype(jnp.bfloat16)


def scatter_tp(part, first, half, fill, bufs, sems):
    uq, uh, vq, vh = bufs
    quarter = half // 2

    def rows(h, piece):
        lo = first + h * half
        a, b = {"h": (lo, lo + half), "q1": (lo, lo + quarter), "q2": (lo + quarter, lo + half)}[piece]
        return slice(a, b)

    def spot(h, f, g, piece):
        return part.at[slot_of(h, f, g), rows(h, piece), :]

    names = ("q1", "q2", "h", "h")
    offs = (2, 2, 1, 3)

    def u_move(h, f, kind):
        dst = uq.at[h, f, kind] if kind < 2 else uh.at[h, f, kind - 2]
        src = spot(h, f, offs[kind], names[kind])
        return remote(src, dst, (sems[0].at[h], sems[1].at[h]), f * 4 + kind, g_peer(h, 1 if kind % 2 == 0 else 3))

    def v_move(h, kind):
        dst = vq.at[h, kind] if kind < 2 else vh.at[h, kind - 2]
        src = spot(h, offs[kind], 0, names[kind])
        return remote(src, dst, (sems[0].at[h], sems[1].at[h]), 16 + kind, f_peer(h, 1 if kind % 2 == 0 else 3))

    def each(fn):
        for h in (0, 1):
            lax.fori_loop(0, 4, lambda f, _, h=h: (fn(h, f), 0)[1], 0)

    def step1():
        def far_rows(f, _):
            fill(slot_of(0, f, 2))
            u_move(0, f, 0).start()
            u_move(0, f, 1).start()
            return 0

        lax.fori_loop(0, 4, far_rows, 0)
        for f in (2, 0, 1, 3):
            if f != 2:
                fill(slot_of(1, f, 2))
            u_move(1, f, 0).start()
            u_move(1, f, 1).start()

    def made():
        def near(i, _):
            f, g = i // 3 + i // 6, i % 3 + i % 3 // 2
            fill(slot_of(0, f, g))
            return 0

        lax.fori_loop(0, 9, near, 0)

    def pass_on(h, f):
        for kind, g, piece in ((0, 1, "q1"), (1, 3, "q2")):
            u_move(h, f, kind).wait_recv()
            add_to(spot(h, f, g, piece), uq.at[h, f, kind])
            u_move(h, f, kind + 2).start()

    def summed(h, f):
        u_move(h, f, 2).wait_recv()
        u_move(h, f, 3).wait_recv()
        add_to(spot(h, f, 0, "h"), uh.at[h, f, 0], uh.at[h, f, 1])

    def far():
        for h in (0, 1):
            summed(h, 2)
            v_move(h, 0).start()
            v_move(h, 1).start()

    def sides():
        for f, kind, piece in ((1, 0, "q1"), (3, 1, "q2")):
            for h in (0, 1):
                summed(h, f)
                v_move(h, kind).wait_recv()
                add_to(spot(h, f, 0, piece), vq.at[h, kind])
                v_move(h, kind + 2).start()

    def own():
        for h in (0, 1):
            summed(h, 0)

    def last():
        for h in (0, 1):
            v_move(h, 2).wait_recv()
            v_move(h, 3).wait_recv()
            add_to(spot(h, 0, 0, "h"), vh.at[h, 0], vh.at[h, 1])

    def finish():
        def u_sent(h, f):
            for kind in range(4):
                u_move(h, f, kind).wait_send()

        each(u_sent)
        for h in (0, 1):
            for kind in range(4):
                v_move(h, kind).wait_send()

    return [step1, made, lambda: each(pass_on), far, sides, own, last], finish


def sum_bufs(half):
    b16, q = jnp.bfloat16, half // 2
    return [
        VMEM((2, 4, 2, q, 256), b16), VMEM((2, 4, 2, half, 256), b16), VMEM((2, 2, q, 256), b16), VMEM((2, 2, half, 256), b16)
    ]


def gather_seq(own, block, sems):
    s, _, _, _ = here()
    z, core = s // 2, s % 2

    def slot(dz, other=0):
        return (z + dz) % 4 * 2 + (core + other) % 2

    rows = {"q1": slice(0, 256), "q2": slice(256, 512), "all": slice(0, 512)}
    plan = [
        (0, "q1", 1), (0, "q2", 3), (0, "q2", 1), (0, "q1", 3), (3, "q1", 1), (1, "q2", 3),
        (0, "all", 0), (3, "all", 0), (1, "all", 0), (2, "q1", 0), (2, "q2", 0),
    ]

    def copy(kind, arriving):
        dz, piece, step = plan[kind]
        k = slot((dz - step) % 4, 0 if step else 1) if arriving else slot(dz)
        dst = block(k, rows[piece])
        src = own.at[rows[piece], :] if dz == 0 and not arriving else dst
        peer = slot(step) if step else slot(0, 1)
        return remote(src, dst, sems, kind, {"seq": peer})

    def send(*kinds):
        for kind in kinds:
            copy(kind, False).start()

    def wait(*kinds):
        for kind in kinds:
            copy(kind, True).wait_recv()

    def finish():
        for kind in range(11):
            copy(kind, False).wait_send()

    return slot, send, wait, finish


ORDER = (0, 1, 7, 2, 6, 3, 5, 4)


def layer(
    hidden, gain, conv_w, conv_b, x_proj, dt_w, dt_b, a_log, skip, ssm_state, ids, gates, moe_gain,
    in_x, in_z, out_w, gate_hbm, up_hbm, down_hbm,
    out,
    resid, first, scaled, xs, zs, u, share, heard, proj, step, dtx, bt, y, states, gated, terms, tq, th, tvq, tvh,
    gate_w, up_w, down_w, outgoing, full, normed, active, parts, back, places, pq, ph, pvq, pvh, rq, rh, rvq, rvh,
    l_sem, h_sem, w_send, w_recv, f_send, f_recv, r_send, r_recv, c_send, c_recv, s_send, s_recv, t_send, t_recv,
    e_sem, g_send, g_recv, p_send, p_recv, a_send, a_recv, b_send, b_recv,
):
    s, t, _, _ = here()
    def beside(ref):
        return lambda k, rows: ref.at[rows, pl.ds(pl.multiple_of(k * 512, 512), 512)]

    def stacked(ref):
        return lambda k, rows: ref.at[pl.ds(pl.multiple_of(k * 512 + rows.start, 256), rows.stop - rows.start), 0:512]

    x_block, z_block, o_block = beside(normed), beside(down_w), stacked(gate_w)
    kept = up_w.at[:, 0:512]
    fetch = [
        pltpu.make_async_copy(src.at[0], dst, e_sem.at[i])
        for i, (src, dst) in enumerate(((gate_hbm, gate_w), (up_hbm, up_w), (down_hbm, down_w)))
    ]
    loads = [
        pltpu.make_async_copy(src, block(s, slice(0, 512)), l_sem.at[i])
        for i, (src, block) in enumerate(((in_x, x_block), (in_z, z_block), (out_w, o_block)))
    ]
    for load in loads:
        load.start()
    first[t, 16:272, :] = hidden[...]
    name = lax.broadcasted_iota(jnp.int32, (16, 256), 0)
    either = jnp.where((name == ids[0:1, :]) | (name == ids[1:2, :]), 1.0, 0.0).astype(jnp.bfloat16)
    row = lax.broadcasted_iota(jnp.int32, (256, 256), 0)
    col = lax.broadcasted_iota(jnp.int32, (256, 256), 1)
    before = jnp.where(row < col, 1.0, 0.0).astype(jnp.bfloat16)
    slots = jnp.dot(either, before, preferred_element_type=jnp.float32)
    line = lax.broadcasted_iota(jnp.int32, (768, 256), 0).astype(jnp.float32)

    def place(k):
        mine = ids[k : k + 1, :]
        target = jnp.sum(jnp.where(name == mine, slots, 0.0), axis=0, keepdims=True) + 96.0 * mine.astype(jnp.float32)
        return jnp.where(line == target, 1.0, 0.0)

    places[0] = place(0).astype(jnp.bfloat16)
    places[1] = place(1).astype(jnp.bfloat16)
    greet(range(1, 8), [(t + d) % 16 for d in range(1, 16)])

    slot, x_send, x_wait, x_done = gather_seq(in_x, x_block, (w_send.at[0], w_recv.at[0]))
    _, z_send, z_wait, z_done = gather_seq(in_z, z_block, (w_send.at[1], w_recv.at[1]))
    _, o_send, o_wait, o_done = gather_seq(out_w, o_block, (w_send.at[2], w_recv.at[2]))

    halo = remote(hidden.at[240:256, :], first.at[t, 0:16, :], (h_sem.at[0], h_sem.at[1]), 0, {"seq": (s + 1) % 8})
    halo.start()
    x_send(0, 1, 2, 3)
    stages, gathered = gather_tp(first, ((144, 208, 272), (0, 80, 144)), (f_send, f_recv), halo.wait_recv)
    stages[0]()
    x_send(6)
    for stage in stages[1:4]:
        stage()
    x_wait(0)
    x_send(4)
    x_wait(1)
    x_send(5)
    for stage in stages[4:]:
        stage()

    x_wait(2, 3)
    x_send(7, 8)
    z_send(0, 1, 2, 3, 6)

    def squares(k, total):
        wide = first[k].astype(jnp.float32)
        wide = wide * wide
        return total + (wide[:, 0:128] + wide[:, 128:256])

    total = lax.fori_loop(0, 16, squares, jnp.zeros((272, 128), jnp.float32))
    scale = lax.rsqrt(jnp.sum(total, axis=1, keepdims=True) * (1.0 / 4096.0) + EPS)

    def norm(k, _):
        cols = pl.ds(pl.multiple_of(k * 256, 256), 256)
        scaled[:, cols] = (first[k].astype(jnp.float32) * scale * gain[:, cols]).astype(jnp.bfloat16)
        return 0

    lax.fori_loop(0, 16, norm, 0)

    def product(total, top, weight, k):
        cols = pl.ds(pl.multiple_of(k * 512, 512), 512)
        term = jnp.dot(scaled[top:272, cols], weight(k, slice(0, 512))[...], preferred_element_type=jnp.float32)
        total[...] = total[...] + term

    xs[...] = jnp.zeros_like(xs)
    loads[0].wait()
    product(xs, 0, x_block, slot(0))
    product(xs, 0, x_block, slot(3))
    product(xs, 0, x_block, slot(1))
    x_wait(4, 5)
    x_send(9, 10)
    o_send(0, 1, 2, 3, 6)
    product(xs, 0, x_block, slot(2))
    x_wait(6, 7, 8)
    for dz in (0, 3, 1):
        product(xs, 0, x_block, slot(dz, 1))
    x_wait(9, 10)
    product(xs, 0, x_block, slot(2, 1))

    xs[...] = xs[...].astype(jnp.bfloat16).astype(jnp.float32)
    xs[0:16, :] = jnp.where(s > 0, xs[0:16, :], 0.0)
    total = conv_b[...]
    for tap in range(4):
        total = total + conv_w[tap : tap + 1, :] * xs[13 + tap : 269 + tap, :]
    u[...] = silu(total).astype(jnp.bfloat16)

    def projection(first, end):
        return lax.dot_general(
            u[...], x_proj[first:end, :], (((1,), (1,)), ((), ())), preferred_element_type=jnp.float32
        ).astype(jnp.bfloat16)

    low, rest = projection(0, 512), projection(512, 544)
    rest = jnp.concatenate([rest, jnp.zeros((256, 96), jnp.bfloat16)], axis=1)
    for g in range(16):
        share[g, :, 0:512] = low[16 * g : 16 * g + 16, :]
        share[g, :, 512:640] = rest[16 * g : 16 * g + 16, :]

    def give(d, arriving=False):
        peer = (t + d) % 16
        k = (t + 16 - d) % 16 if arriving else t
        return remote(share.at[peer], heard.at[k], (r_send, r_recv), d, {"tp": peer})

    def tell(d, arriving=False):
        peer = (t + d) % 16
        k = (t + 16 - d) % 16 if arriving else t
        return remote(proj.at[k], proj.at[k], (c_send, c_recv), d, {"tp": peer})

    def others(fn, count=16):
        lax.fori_loop(1, count, lambda d, _: (fn(d), 0)[1], 0)

    others(lambda d: give(d).start())
    heard[t] = share[t]
    others(lambda d: give(d, True).wait_recv())
    proj[t] = lax.fori_loop(
        0, 16, lambda k, total: total + heard[k].astype(jnp.float32), jnp.zeros((16, 640), jnp.float32)
    ).astype(jnp.bfloat16)
    others(lambda d: tell(d).start())
    z_wait(0)
    z_send(4)
    z_wait(1)
    z_send(5)
    others(lambda d: tell(d, True).wait_recv())
    z_wait(2, 3)
    z_send(7, 8)
    o_wait(0)
    o_send(4)
    o_wait(1)
    o_send(5)

    low = proj[:, :, 0:512].reshape(256, 512)
    bc = proj[:, :, 512:640].reshape(256, 128).astype(jnp.float32)
    size = softplus(jnp.dot(low, dt_w[...], preferred_element_type=jnp.float32) + dt_b[...])
    step[...] = size
    dtx[...] = size * u[...].astype(jnp.float32)
    spread_b(bc, bt)
    rate = jnp.exp(a_log[...]) * (-LOG2E)
    states[s, 0:16, :] = jnp.exp2(rate * jnp.sum(size, axis=0, keepdims=True)).astype(jnp.bfloat16)
    states[s, 16:32, :] = run_states(step, dtx, bt, rate, jnp.zeros((16, 512), jnp.float32), None).astype(jnp.bfloat16)

    def pass_on(d, arriving=False):
        k = (s + 8 - d) % 8 if arriving else s
        return remote(states.at[k], states.at[k], (s_send, s_recv), d, {"seq": (s + d) % 8})

    lax.fori_loop(1, 8 - s, lambda d, _: (pass_on(d).start(), 0)[1], 0)
    zs[...] = jnp.zeros_like(zs)
    loads[1].wait()
    for dz in (0, 3, 1):
        product(zs, 16, z_block, slot(dz))
    z_wait(4, 5)
    z_send(9, 10)
    lax.fori_loop(1, s + 1, lambda d, _: (pass_on(d, True).wait_recv(), 0)[1], 0)

    def enter(k, state):
        return states[k, 0:16, :].astype(jnp.float32) * state + states[k, 16:32, :].astype(jnp.float32)

    start = lax.fori_loop(0, s, enter, ssm_state[...])
    run_states(step, dtx, bt, rate, start, kept)
    o_wait(2, 3)
    o_send(7, 8)
    c = block_c(bc)
    for g in range(16):
        y[16 * g : 16 * g + 16, :] = jnp.dot(
            c[16 * g : 16 * g + 16, :], kept[256 * g : 256 * g + 256, :], preferred_element_type=jnp.float32
        )
    fetch[1].start()
    z_wait(6, 7, 8, 9, 10)
    product(zs, 16, z_block, slot(2))
    for dz in range(4):
        product(zs, 16, z_block, slot(dz, 1))
    z_done()
    fetch[2].start()
    gate = silu(zs[...].astype(jnp.bfloat16).astype(jnp.float32))
    gated[...] = ((y[...] + skip[...] * u[...].astype(jnp.float32)) * gate).astype(jnp.bfloat16)
    loads[2].wait()
    o_wait(4, 5)
    o_send(9, 10)
    o_wait(6, 7, 8, 9, 10)

    def fill_terms(k):
        rows = pl.ds(pl.multiple_of(k // 2 * 512, 512), 512)
        cols = pl.ds(pl.multiple_of(k % 2 * 256, 256), 256)
        terms[k] = jnp.dot(gated[...], gate_w[rows, cols], preferred_element_type=jnp.float32).astype(jnp.bfloat16)

    stages, terms_done = scatter_tp(terms, 0, 128, fill_terms, (tq, th, tvq, tvh), (t_send, t_recv))
    stages[0]()
    stages[1]()
    o_done()
    fetch[0].start()
    for stage in stages[2:]:
        stage()
    resid[...] = (hidden[...].astype(jnp.float32) + terms[t].astype(jnp.float32)).astype(jnp.bfloat16)


    outgoing[...] = jnp.dot(places[0] + places[1], resid[...], preferred_element_type=jnp.float32).astype(jnp.bfloat16)

    def mine(ref, k):
        return ref.at[pl.ds(pl.multiple_of(k * 96, 16), 96), :]

    def there(i):
        d = ORDER[i]
        peer = (s + d) % 8
        return remote(mine(outgoing, peer), mine(full.at[t], i), (a_send, a_recv), i, {"seq": peer})

    for i in range(1, 8):
        there(i).start()
    full[t, 0:96, :] = mine(outgoing, s)[...]

    spread, spread_done = zip(
        *[
            gather_tp(
                full,
                ((c * 384, c * 384 + 96, c * 384 + 192), (c * 384 + 192, c * 384 + 288, c * 384 + 384)),
                (g_send.at[c], g_recv.at[c]),
            )
            for c in (0, 1)
        ]
    )

    def chunk_norm(c):
        rows = slice(c * 384, c * 384 + 384)

        def squares(k, total):
            wide = full[k, rows, :].astype(jnp.float32)
            wide = wide * wide
            return total + (wide[:, 0:128] + wide[:, 128:256])

        total = lax.fori_loop(0, 16, squares, jnp.zeros((384, 128), jnp.float32))
        scale = lax.rsqrt(jnp.sum(total, axis=1, keepdims=True) * (1.0 / 4096.0) + EPS)

        def apply(k, _):
            cols = pl.ds(pl.multiple_of(k * 256, 256), 256)
            normed[rows, cols] = (full[k, rows, :].astype(jnp.float32) * scale * moe_gain[:, cols]).astype(jnp.bfloat16)
            return 0

        lax.fori_loop(0, 16, apply, 0)

    def hidden_units(c, j):
        rows, cols = slice(c * 384, c * 384 + 384), slice(j * 256, j * 256 + 256)
        a = jnp.dot(normed[rows, :], gate_w[:, cols], preferred_element_type=jnp.float32)
        b = jnp.dot(normed[rows, :], up_w[:, cols], preferred_element_type=jnp.float32)
        active[rows, cols] = (silu(a) * b).astype(jnp.bfloat16)

    def fill_parts(c):
        rows = slice(c * 384, c * 384 + 384)

        def fill(slot):
            cols = pl.ds(pl.multiple_of(slot * 256, 256), 256)
            parts[slot, rows, :] = jnp.dot(
                active[rows, :], down_w[:, cols], preferred_element_type=jnp.float32
            ).astype(jnp.bfloat16)

        return fill

    sums = ((pq, ph, pvq, pvh), (rq, rh, rvq, rvh))
    part, part_done = zip(
        *[scatter_tp(parts, c * 384, 192, fill_parts(c), sums[c], (p_send.at[c], p_recv.at[c])) for c in (0, 1)]
    )

    def home(i):
        peer = (s + 8 - ORDER[i]) % 8
        return remote(mine(parts.at[t], i), mine(back, s), (b_send, b_recv), i, {"seq": peer})

    def run(stages, *which):
        for i in which:
            stages[i]()

    for i in (1, 2, 3):
        there(i).wait_recv()
    run(spread[0], 0, 1)
    for i in (4, 5, 6, 7):
        there(i).wait_recv()
    run(spread[1], 0)
    run(spread[0], 2, 3)
    run(spread[1], 1)
    run(spread[0], 4)
    run(spread[1], 2)
    run(spread[0], 5)
    run(spread[1], 3)
    run(spread[0], 6)
    x_done()
    chunk_norm(0)
    run(spread[1], 4)
    fetch[0].wait()
    fetch[1].wait()
    hidden_units(0, 0)
    run(spread[1], 5)
    hidden_units(0, 1)
    hidden_units(0, 2)
    fetch[2].wait()
    run(part[0], 0)
    run(spread[1], 6)
    run(part[0], 1, 2)
    chunk_norm(1)
    hidden_units(1, 0)
    run(part[0], 3)
    hidden_units(1, 1)
    run(part[0], 4)
    hidden_units(1, 2)
    run(part[1], 0)
    run(part[0], 5, 6)
    for i in (1, 2, 3):
        home(i).start()
    mine(back, s)[...] = parts[t, 0:96, :]
    run(part[1], 1, 2, 3, 4, 5, 6)
    for i in (4, 5, 6, 7):
        home(i).start()
    fine = [gates[k : k + 1, :] for k in (0, 1)]
    high = [g.astype(jnp.bfloat16).astype(jnp.float32) for g in fine]
    result = resid[...].astype(jnp.float32)
    wide = [places[k].astype(jnp.float32) for k in (0, 1)]
    weigh = [
        (wide[0] * g[0] + wide[1] * g[1]).astype(jnp.bfloat16) for g in (high, [fine[k] - high[k] for k in (0, 1)])
    ]
    for i in range(1, 8):
        home(i).wait_recv()
    for w in weigh:
        result = result + lax.dot_general(
            w, back[...], (((0,), (0,)), ((), ())), preferred_element_type=jnp.float32
        )
    out[...] = result.astype(jnp.bfloat16)

    for c in (0, 1):
        spread_done[c]()
        part_done[c]()
    for i in range(1, 8):
        there(i).wait_send()
        home(i).wait_send()
    halo.wait_send()
    gathered()
    others(lambda d: give(d).wait_send())
    others(lambda d: tell(d).wait_send())
    lax.fori_loop(1, 8 - s, lambda d, _: (pass_on(d).wait_send(), 0)[1], 0)
    terms_done()


def call_layer(*args):
    vm, hbm = pl.BlockSpec(memory_space=pltpu.VMEM), pl.BlockSpec(memory_space=pl.ANY)
    b16, wide = jnp.bfloat16, jnp.float32
    dma = pltpu.SemaphoreType.DMA
    return pl.pallas_call(
        layer,
        out_shape=bf16(256, 256),
        in_specs=[vm] * 13 + [hbm] * 6,
        out_specs=vm,
        scratch_shapes=[
            VMEM((256, 256), b16), VMEM((16, 272, 256), b16), VMEM((272, 4096), b16), VMEM((272, 512), wide),
            VMEM((256, 512), wide), VMEM((256, 512), b16), VMEM((16, 16, 640), b16), VMEM((16, 16, 640), b16),
            VMEM((16, 16, 640), b16), VMEM((256, 512), wide), VMEM((256, 512), wide), VMEM((16, 16, 128), wide),
            VMEM((256, 512), wide), VMEM((8, 32, 512), b16), VMEM((256, 512), b16), VMEM((16, 256, 256), b16),
            *sum_bufs(128),
            VMEM((4096, 768), b16), VMEM((4096, 768), b16), VMEM((768, 4096), b16),
            VMEM((768, 256), b16), VMEM((16, 768, 256), b16), VMEM((768, 4096), b16),
            VMEM((768, 768), b16), VMEM((16, 768, 256), b16), VMEM((768, 256), b16), VMEM((2, 768, 256), b16),
            *sum_bufs(192), *sum_bufs(192),
            dma((3,)), dma((2, 1)), dma((3, 11)), dma((3, 11)), dma((2, 20)), dma((2, 20)), dma((16,)), dma((16,)),
            dma((16,)), dma((16,)), dma((8,)), dma((8,)), dma((2, 20)), dma((2, 20)),
            dma((3,)), dma((2, 2, 20)), dma((2, 2, 20)), dma((2, 2, 20)), dma((2, 2, 20)),
            dma((8,)), dma((8,)), dma((8,)), dma((8,)),
        ],
        compiler_params=pltpu.CompilerParams(collective_id=1, has_side_effects=True, vmem_limit_bytes=62 << 20),
    )(*args)


def local(
    hidden,
    expert_ids,
    expert_gates,
    mamba_gain,
    in_x_weight,
    in_z_weight,
    conv_weight,
    conv_bias,
    x_proj_weight,
    dt_weight,
    dt_bias,
    a_log,
    skip,
    ssm_state,
    out_weight,
    moe_gain,
    expert_gate,
    expert_up,
    expert_down,
):
    return call_layer(
        hidden, mamba_gain[None], conv_weight, conv_bias[None], x_proj_weight.T, dt_weight, dt_bias[None], a_log, skip[None],
        ssm_state, expert_ids.T, expert_gates.T, moe_gain[None], in_x_weight, in_z_weight, out_weight, expert_gate,
        expert_up, expert_down,
    )


def solution(mesh):
    placed = (
        P("seq", "tp"),
        P("seq", None),
        P("seq", None),
        P(),
        P("seq", "tp"),
        P("seq", "tp"),
        P(None, "tp"),
        P("tp"),
        P("tp", None),
        P(None, "tp"),
        P("tp"),
        P(None, "tp"),
        P("tp"),
        P(None, "tp"),
        P("tp", "seq"),
        P(),
        P("seq", None, "tp"),
        P("seq", None, "tp"),
        P("seq", "tp", None),
    )
    return jax.shard_map(local, mesh=mesh, in_specs=placed, out_specs=P("seq", "tp"), check_vma=False)
```
